128 devices in a mesh: instance: 4 (over x), layout: 4 (over y), tensor: 8 (over z, core).
Axes of the slice: x: 4, y: 4, z: 4, core: 2. Of those that a mesh axis runs over, the one named last changes fastest.
Arguments:
- prefill_pool: bfloat16 [4608, 2, 8, 64, 128], P(('instance', 'layout', 'tensor')), may hold values from -6 to 6
- lengths: int32 [16], replicated, may hold values from 10240 to 32768, as said below
- src_table: int32 [16, 512], replicated, may hold values from 0 to 4607, as said below
- dst_table: int32 [16, 512], replicated, may hold values from 0 to 4607, as said below
- row_request: int32 [64], replicated, may hold values from 0 to 15, as said below
- positions: int32 [64], replicated, may hold values from 1 to 32768, as said below
- queries: bfloat16 [4, 64, 16384], P(None, 'instance', 'tensor'), may hold values from -80 to 80
- step_key_value: bfloat16 [4, 64, 2, 8, 128], P(None, 'instance', None, 'tensor'), may hold values from -6 to 6
- out_weight: bfloat16 [16384, 16384], P('tensor', ('instance', 'layout')), may hold values from -0.046875 to 0.046875
- residual: bfloat16 [4, 64, 16384], P(None, None, ('instance', 'layout', 'tensor')), may hold values from -4 to 4
Outputs:
- decode_pool: bfloat16 [4608, 2, 8, 64, 128], P(('instance', 'layout'), None, 'tensor')
- attn_out: float32 [4, 64, 16384], P(None, None, ('instance', 'layout', 'tensor'))
The draws below stay inside these ranges and needn't reach their ends.
Inputs may be any that keep to these rules, and one draw needn't show every extreme that they name: `lengths`: exactly one request has 32768 tokens; every other has at most 12288. `src_table`: each request r is prefilled by one instance group p(r): its live pages name distinct rows of prefill_pool, page j on the device of group p(r) with layout index j mod 4 and tensor index (j // 4) mod 8; so one device holds at most 16 live pages of one request. Entries of pages that are not live name some row of group p(r). The pairs (p(r), g(r)) with g(r) of dst_table are all distinct. `dst_table`: each request r is decoded by one instance group g(r): its live pages name distinct rows of decode_pool on the devices of that group, page j on layout index j mod 4. Entries of pages that are not live name some row of group g(r). `row_request`: the rows of instance index i (rows i * 16 onward) belong to the requests that group i decodes, 4 rows each. `positions`: at most the length of the row's request; one row of every request sees its whole prompt.
All inputs are finite; a program needn't handle non-finite values.
Results may differ from the reference program's by a relative error of at most 0.00305.
Values may be sent and summed in bfloat16 or wider, within the bound.
A program may use at most 128 MiB of HBM per device.

```python
import jax
import jax.numpy as jnp
from jax import lax

D = 16384
QUERY_HEADS = 128
KEY_VALUE_HEADS = 8
HEAD_SIZE = 128
PAGE_TOKENS = 64
MAXLEN = 32768
OTHERLEN = 12288
DECODE_STEPS = 4
REQUEST_ROWS = 4
PROMPT_PAGES = 512
REQUEST_COUNT = 16
STEP_ROWS = 64
SRC_DEV = 36
PREFILL_SLOTS = 4608
DST_DEV = 288
DECODE_SLOTS = 4608
N_INSTANCE = 4
N_LAYOUT = 4
N_TENSOR = 8


def plan(key):
    pairs = jax.random.permutation(jax.random.fold_in(key, 101), REQUEST_COUNT).astype(jnp.int32)
    prod = pairs // N_INSTANCE
    dec = pairs % N_INSTANCE
    others = jax.random.randint(jax.random.fold_in(key, 102), (REQUEST_COUNT,), OTHERLEN * 5 // 6, OTHERLEN + 1)
    longest = jax.random.randint(jax.random.fold_in(key, 103), (), 0, REQUEST_COUNT)
    lengths = jnp.where(jnp.arange(REQUEST_COUNT) == longest, MAXLEN, others).astype(jnp.int32)
    return (pairs, prod, dec, lengths)


def place_pages(shift_key, home, order_by, lengths, spread, per_dev, n_dev, device):
    pages = (lengths + PAGE_TOKENS - 1) // PAGE_TOKENS
    most = (pages + spread - 1) // spread
    before = (home[None, :] == home[:, None]) & (order_by[None, :] < order_by[:, None])
    offset = jnp.sum(jnp.where(before, most[None, :], 0), axis=1)
    steps_k = jnp.arange(PROMPT_PAGES, dtype=jnp.int32) // spread
    shift = jax.random.randint(shift_key, (n_dev,), 0, per_dev)
    slot = (offset[:, None] + steps_k[None, :] + shift[device]) % per_dev
    return (device * per_dev + slot).astype(jnp.int32)


def rows_plan(key, shared):
    pairs, prod, dec, lengths = shared
    owner = jnp.argsort(pairs, stable=True).astype(jnp.int32)
    group_rows = N_INSTANCE * REQUEST_ROWS
    key_rows = jax.random.split(jax.random.fold_in(key, 104), N_INSTANCE)
    perms = jax.vmap(lambda k: jax.random.permutation(k, group_rows))(key_rows)
    member = perms // REQUEST_ROWS
    groups = jnp.arange(N_INSTANCE, dtype=jnp.int32)[:, None]
    request = owner[member * N_INSTANCE + groups].reshape(-1).astype(jnp.int32)
    first = (perms % REQUEST_ROWS == 0).reshape(-1)
    return (request, first)


def draw_lengths(key, part):
    shared = plan(key)
    return shared[3]


def draw_src_table(key, part):
    shared = plan(key)
    key = jax.random.fold_in(key, 2)
    pairs, prod, dec, lengths = shared
    page_ids = jnp.arange(PROMPT_PAGES, dtype=jnp.int32)
    device = (prod[:, None] * N_LAYOUT + page_ids[None, :] % N_LAYOUT) * N_TENSOR + page_ids[None, :] // N_LAYOUT % N_TENSOR
    return place_pages(key, prod, dec, lengths, N_LAYOUT * N_TENSOR, SRC_DEV, N_INSTANCE * N_LAYOUT * N_TENSOR, device)


def draw_dst_table(key, part):
    shared = plan(key)
    key = jax.random.fold_in(key, 3)
    pairs, prod, dec, lengths = shared
    page_ids = jnp.arange(PROMPT_PAGES, dtype=jnp.int32)
    device = dec[:, None] * N_LAYOUT + page_ids[None, :] % N_LAYOUT
    return place_pages(key, dec, prod, lengths, N_LAYOUT, DST_DEV, N_INSTANCE * N_LAYOUT, device)


def draw_row_request(key, part):
    shared = plan(key)
    request, first = rows_plan(key, shared)
    return request


def draw_positions(key, part):
    shared = plan(key)
    request, first = rows_plan(key, shared)
    key = jax.random.fold_in(key, 5)
    seen = shared[3][request]
    drawn = jax.random.randint(key, (STEP_ROWS,), 1, seen + 1)
    return jnp.where(first, seen, drawn).astype(jnp.int32)


def draw_queries(key, part):
    key = jax.random.fold_in(key, 7)
    shape = (DECODE_STEPS, STEP_ROWS, QUERY_HEADS * HEAD_SIZE)
    base = jax.random.normal(key, shape, jnp.float32)
    return jnp.clip(base, -6.0, 6.0).astype(jnp.bfloat16)


def steps_of(own_key, shape, shards, low, high):
    gain, own = 1.0, jax.random.fold_in(own_key, 6)
    for dim, blocks in shards:
        heights = jnp.exp(jax.random.uniform(jax.random.fold_in(own, dim), (blocks,), jnp.float32, low / len(shards), high / len(shards)))
        gain = gain * jnp.repeat(heights, shape[dim] // blocks).reshape([-1 if axis == dim else 1 for axis in range(len(shape))])
    return gain


def normal_values(own_key, extent, deviation, most, cuts=(), kind=jnp.bfloat16):
    values = jax.random.normal(own_key, extent, jnp.float32) * deviation
    if len(cuts) > 0:
        values = steps_of(own_key, extent, cuts, -0.22, 0.18) * values
    return jnp.clip(values, min=-most, max=most).astype(kind)


def setup_inputs(seed: int = 0) -> dict:
    arg_keys = jax.random.split(jax.random.key(seed), 11)
    return {
        "prefill_pool": normal_values(arg_keys[0], (PREFILL_SLOTS, 2, KEY_VALUE_HEADS, PAGE_TOKENS, HEAD_SIZE), 1.0, 6.0, ((0, 128),)),
        "lengths": draw_lengths(jax.random.fold_in(arg_keys[10], 71), 0),
        "src_table": draw_src_table(jax.random.fold_in(arg_keys[10], 71), 0),
        "dst_table": draw_dst_table(jax.random.fold_in(arg_keys[10], 71), 0),
        "row_request": draw_row_request(jax.random.fold_in(arg_keys[10], 71), 0),
        "positions": draw_positions(jax.random.fold_in(arg_keys[10], 71), 0),
        "queries": draw_queries(jax.random.fold_in(arg_keys[10], 71), 0),
        "step_key_value": normal_values(arg_keys[7], (DECODE_STEPS, STEP_ROWS, 2, KEY_VALUE_HEADS, HEAD_SIZE), 1.0, 6.0, ((1, 4), (3, 8))),
        "out_weight": normal_values(arg_keys[8], (QUERY_HEADS * HEAD_SIZE, D), (QUERY_HEADS * HEAD_SIZE) ** -0.5, 0.046875, ((0, 8), (1, 16))),
        "residual": normal_values(arg_keys[9], (DECODE_STEPS, STEP_ROWS, D), 0.5, 4.0, ((2, 128),)),
    }


def reference(prefill_pool, lengths, src_table, dst_table, row_request, positions, queries, step_key_value, out_weight, residual):
    grouped_query = QUERY_HEADS // KEY_VALUE_HEADS
    npages = (lengths + PAGE_TOKENS - 1) // PAGE_TOKENS
    page_ids = jnp.arange(PROMPT_PAGES, dtype=jnp.int32)

    def migrate_pages(r, pool):
        live = page_ids < npages[r]
        target = jnp.where(live, dst_table[r], DECODE_SLOTS).astype(jnp.int32)
        return pool.at[target].set(prefill_pool[src_table[r]], mode="drop")

    decode_pool = lax.fori_loop(0, REQUEST_COUNT, migrate_pages, jnp.zeros((DECODE_SLOTS, 2, KEY_VALUE_HEADS, PAGE_TOKENS, HEAD_SIZE), jnp.bfloat16))
    order = jnp.argsort(row_request, stable=True).astype(jnp.int32).reshape(REQUEST_COUNT, REQUEST_ROWS)
    scale = HEAD_SIZE ** -0.5
    causal = jnp.arange(DECODE_STEPS)[:, None] >= jnp.arange(DECODE_STEPS)[None, :]
    token_ids = jnp.arange(PROMPT_PAGES * PAGE_TOKENS, dtype=jnp.int32)

    def attend(r):
        decode_rows = order[r]
        paged_attention = prefill_pool[src_table[r]]
        key_rows = paged_attention[:, 0].transpose(1, 0, 2, 3).reshape(KEY_VALUE_HEADS, PROMPT_PAGES * PAGE_TOKENS, HEAD_SIZE).astype(jnp.float32)
        value_rows = paged_attention[:, 1].transpose(1, 0, 2, 3).reshape(KEY_VALUE_HEADS, PROMPT_PAGES * PAGE_TOKENS, HEAD_SIZE).astype(jnp.float32)
        query_vector = queries[:, decode_rows].astype(jnp.float32).reshape(DECODE_STEPS, REQUEST_ROWS, KEY_VALUE_HEADS, grouped_query, HEAD_SIZE).transpose(2, 0, 1, 3, 4)
        cached = jnp.einsum("ksrgd,ktd->ksrgt", query_vector, key_rows) * scale
        seen = token_ids[None, :] < positions[decode_rows][:, None]
        cached = jnp.where(seen[None, None, :, None, :], cached, -jnp.inf)
        fresh_k = step_key_value[:, decode_rows, 0].astype(jnp.float32)
        fresh_v = step_key_value[:, decode_rows, 1].astype(jnp.float32)
        fresh = jnp.einsum("ksrgd,urkd->ksrgu", query_vector, fresh_k) * scale
        fresh = jnp.where(causal[None, :, None, None, :], fresh, -jnp.inf)
        top = jnp.maximum(jnp.max(cached, axis=-1), jnp.max(fresh, axis=-1))
        w_cached = jnp.exp(cached - top[..., None])
        w_fresh = jnp.exp(fresh - top[..., None])
        total = jnp.sum(w_cached, axis=-1) + jnp.sum(w_fresh, axis=-1)
        r_cached = lax.optimization_barrier(w_cached.astype(jnp.bfloat16)).astype(jnp.float32)
        r_fresh = lax.optimization_barrier(w_fresh.astype(jnp.bfloat16)).astype(jnp.float32)
        numer = jnp.einsum("ksrgt,ktd->ksrgd", r_cached, value_rows) + jnp.einsum("ksrgu,urkd->ksrgd", r_fresh, fresh_v)
        context = numer / total[..., None]
        return context.transpose(1, 2, 0, 3, 4).reshape(DECODE_STEPS, REQUEST_ROWS, QUERY_HEADS * HEAD_SIZE).astype(jnp.bfloat16)

    contexts = lax.map(attend, jnp.arange(REQUEST_COUNT, dtype=jnp.int32))
    flat = contexts.transpose(1, 0, 2, 3).reshape(DECODE_STEPS, STEP_ROWS, QUERY_HEADS * HEAD_SIZE)
    context_all = jnp.zeros((DECODE_STEPS, STEP_ROWS, QUERY_HEADS * HEAD_SIZE), jnp.bfloat16).at[:, order.reshape(-1)].set(flat)
    projected = jnp.dot(context_all.reshape(DECODE_STEPS * STEP_ROWS, QUERY_HEADS * HEAD_SIZE), out_weight, preferred_element_type=jnp.float32)
    attn_out = residual.astype(jnp.float32) + projected.reshape(DECODE_STEPS, STEP_ROWS, D)
    return decode_pool, attn_out
```

```python
import functools

import jax
import jax.numpy as jnp
from jax import lax
from jax.experimental import pallas as pl
from jax.experimental.pallas import tpu as pltpu
from jax.sharding import PartitionSpec as P

MESH = pl.DeviceIdType.MESH
OTHERLEN = 12288
LOW = -1e30
MASKED = -2e30
NI, NL, NT = 4, 4, 8
NEAR = 6
FAR = 10
PAGES = NI * NEAR * NT
EXTRA = FAR * NT


def extra_kernel(p, g, src, dst, send_sem, recv_sem, fill_sem):
    i, l, t = (lax.axis_index(a) for a in ("instance", "layout", "tensor"))
    first = 1 if p == g else 0
    barrier = pltpu.get_barrier_semaphore()

    def peer(group, dt):
        return (group, l, lax.rem(t + dt, NT))

    def copy(k, dt):
        to = peer(g, dt)
        return pltpu.make_async_remote_copy(
            src_ref=src.at[k, :, to[2]],
            dst_ref=dst.at[k, dt],
            send_sem=send_sem.at[dt, k],
            recv_sem=recv_sem.at[dt, k],
            device_id=to,
            device_id_type=MESH,
        )

    @pl.when(i == g)
    def _():
        for dt in range(first, NT):
            pl.semaphore_signal(barrier, inc=1, device_id=peer(p, dt), device_id_type=MESH)

    @pl.when(i == p)
    def _():
        pl.semaphore_wait(barrier, NT - first)

        def send(k, c):
            for dt in range(first, NT):
                copy(k, dt).start()
            return c

        lax.fori_loop(0, FAR, send, 0)

    if p == g:

        @pl.when(i == g)
        def _():
            own = pltpu.make_async_copy(src.at[:, :, t], dst.at[:, 0], fill_sem.at[0])
            own.start()
            own.wait()

    @pl.when(i != g)
    def _():
        fills = [pltpu.make_async_copy(src.at[:, :, h], dst.at[:, h], fill_sem.at[h]) for h in range(NT)]
        for f in fills:
            f.start()
        for f in fills:
            f.wait()

    @pl.when(i == p)
    def _():
        def drain(k, c):
            for dt in range(first, NT):
                copy(k, dt).wait_send()
            return c

        lax.fori_loop(0, FAR, drain, 0)

    @pl.when(i == g)
    def _():
        def arrive(k, c):
            for dt in range(first, NT):
                copy(k, dt).wait_recv()
            return c

        lax.fori_loop(0, FAR, arrive, 0)


def move_extra(p, g, src):
    return pl.pallas_call(
        functools.partial(extra_kernel, p, g),
        out_shape=jax.ShapeDtypeStruct((FAR, NT, 2, 64, 128), jnp.bfloat16),
        in_specs=[pl.BlockSpec(memory_space=pl.ANY)],
        out_specs=pl.BlockSpec(memory_space=pl.ANY),
        scratch_shapes=[
            pltpu.SemaphoreType.DMA((NT, FAR)),
            pltpu.SemaphoreType.DMA((NT, FAR)),
            pltpu.SemaphoreType.DMA((NT,)),
        ],
        compiler_params=pltpu.CompilerParams(collective_id=1 + p * NI + g, has_side_effects=True),
    )(src)


def main_kernel(
    send,
    extra,
    weight,
    query,
    fresh,
    pick,
    order,
    pos,
    pos_x,
    pick_x,
    far,
    residual,
    pages,
    attn,
    recv,
    ext,
    w,
    q,
    qx,
    fkv,
    acc,
    ml,
    got,
    ctx,
    proj,
    red,
    zero,
    send_sem,
    recv_sem,
    own_sem,
    page_sem,
    w_sem,
    ext_sem,
    s1_sem,
    r1_sem,
    s2_sem,
    r2_sem,
    s4_sem,
    r4_sem,
):
    i, l, t = (lax.axis_index(a) for a in ("instance", "layout", "tensor"))
    scale = 128.0**-0.5

    def plane(di, dt):
        return (lax.rem(i + di, NI), l, lax.rem(t + dt, NT))

    def column(di, dl):
        return (lax.rem(i + di, NI), lax.rem(l + dl, NL), t)

    barrier = pltpu.get_barrier_semaphore()
    for di in range(NI):
        for dt in range(NT):
            if di or dt:
                pl.semaphore_signal(barrier, inc=1, device_id=plane(di, dt), device_id_type=MESH)
    for di in range(NI):
        for dl in range(1, NL):
            pl.semaphore_signal(barrier, inc=1, device_id=column(di, dl), device_id_type=MESH)

    w_copy = pltpu.make_async_copy(weight, w, w_sem)
    ext_copy = pltpu.make_async_copy(extra, ext, ext_sem)
    ext_copy.start()
    own = [pltpu.make_async_copy(send.at[0, k, :, t], recv.at[0, k, 0], own_sem.at[k]) for k in range(NEAR)]
    for c in own:
        c.start()
    pl.semaphore_wait(barrier, NI * NT - 1 + NI * (NL - 1))

    def page_copy(k, di, dt):
        to = plane(di, dt)
        return pltpu.make_async_remote_copy(
            src_ref=send.at[di, k, :, to[2]],
            dst_ref=recv.at[di, k, dt],
            send_sem=send_sem.at[di, k, dt],
            recv_sem=recv_sem.at[di, k, dt],
            device_id=to,
            device_id_type=MESH,
        )

    def pair(n):
        di = n % 4
        dz = (di + n // 8) % 4
        return di, dz * 2 + (n // 4) % 2

    def send_page(k, c):
        def one(n, c):
            di, dt = pair(n)

            @pl.when(n != 0)
            def _():
                page_copy(k, di, dt).start()

            return c

        return lax.fori_loop(0, NI * NT, one, c)

    lax.fori_loop(0, NEAR, send_page, 0)
    w_copy.start()

    sorted_q = jnp.dot(pick[...], query[...], preferred_element_type=jnp.float32).astype(jnp.bfloat16)
    sorted_x = jnp.dot(pick_x[...], query[...], preferred_element_type=jnp.float32).astype(jnp.bfloat16)
    fkv[...] = jnp.dot(pick[...], fresh[...], preferred_element_type=jnp.float32).astype(jnp.bfloat16)
    for h in range(16):
        for d in range(NI):
            q[d, h * 16 : (h + 1) * 16, :] = sorted_q[d * 16 : (d + 1) * 16, h * 128 : (h + 1) * 128]
        qx[h * 16 : (h + 1) * 16, :] = sorted_x[:, h * 128 : (h + 1) * 128]
    zero[...] = jnp.zeros_like(zero)

    def update(m, total, weighted, s, v):
        top = jnp.maximum(m, jnp.max(s, axis=1, keepdims=True))
        shrink = jnp.exp(m - top)
        p = jnp.exp(s - top)
        total = total * shrink + jnp.sum(p, axis=1, keepdims=True)
        weighted = weighted * shrink + jnp.dot(p.astype(jnp.bfloat16), v, preferred_element_type=jnp.float32)
        return top, total, weighted

    def dots(a, b):
        return lax.dot_general(a, b, (((1,), (1,)), ((), ())), preferred_element_type=jnp.float32) * scale

    ext_copy.wait()
    ext_out = pltpu.make_async_copy(ext, pages.at[pl.ds(NI * NEAR, FAR)], ext_sem)
    ext_out.start()

    def extra_step(k, carry):
        n = lax.broadcasted_iota(jnp.int32, (1, NT * 64), 1)
        ts = (t + NT - n // 64) % NT
        token = (((NEAR + k) * NT + ts) * NL + l) * 64 + n % 64
        s = dots(qx[...], ext[k, :, 0].reshape(NT * 64, 128))
        s = jnp.where(token < pos_x[...], s, MASKED)
        return update(*carry, s, ext[k, :, 1].reshape(NT * 64, 128))

    empty = (
        jnp.full((256, 1), LOW, jnp.float32),
        jnp.zeros((256, 1), jnp.float32),
        jnp.zeros((256, 128), jnp.float32),
    )
    mx, tx, ax = lax.fori_loop(0, FAR, extra_step, empty)

    a = lax.broadcasted_iota(jnp.int32, (256, 16), 0)
    b = lax.broadcasted_iota(jnp.int32, (256, 16), 1)
    visible = (a % 4 == b % 4) & (b // 4 <= (a // 4) % 4) & (l == 0)
    for d in range(NI):
        rows = slice(d * 16, (d + 1) * 16)
        s = jnp.where(visible, dots(q[d], fkv[rows, :128]), MASKED)
        start = (jnp.maximum(mx + far[d : d + 1, :1], LOW), tx, ax)
        start = (start[0], jnp.where(start[0] > LOW, tx, 0.0), jnp.where(start[0] > LOW, ax, 0.0))
        m, total, weighted = update(*start, s, fkv[rows, 128:])
        acc[d] = weighted
        ml[d, :, :64] = jnp.broadcast_to(m, (256, 64))
        ml[d, :, 64:] = jnp.broadcast_to(total, (256, 64))

    for c in own:
        c.wait()

    def visit(k, c):
        def request(d, c):
            for dt in range(NT):
                if dt:
                    page_copy(k, d, dt).wait_recv()
                else:

                    @pl.when(d != 0)
                    def _():
                        page_copy(k, d, dt).wait_recv()

            pltpu.make_async_copy(recv.at[d, k], pages.at[d * NEAR + k], page_sem.at[d, k]).start()
            n = lax.broadcasted_iota(jnp.int32, (1, NT * 64), 1)
            ts = (t + NT - n // 64) % NT
            token = ((k * NT + ts) * NL + l) * 64 + n % 64
            s = dots(q[d], recv[d, k, :, 0].reshape(NT * 64, 128))
            s = jnp.where(token < pos[d], s, MASKED)
            m, total, weighted = update(
                ml[d, :, :1], ml[d, :, 64:65], acc[d], s, recv[d, k, :, 1].reshape(NT * 64, 128)
            )
            acc[d] = weighted
            ml[d, :, :64] = jnp.broadcast_to(m, (256, 64))
            ml[d, :, 64:] = jnp.broadcast_to(total, (256, 64))
            return c

        return lax.fori_loop(0, NI, request, c)

    lax.fori_loop(0, NEAR, visit, 0)

    joins = []
    for dl in range(1, NL):
        to = column(0, dl)
        for part, ref in enumerate((acc, ml)):
            joins.append(
                pltpu.make_async_remote_copy(
                    src_ref=ref.at[to[1]],
                    dst_ref=got.at[dl - 1, part],
                    send_sem=s1_sem.at[dl - 1, part],
                    recv_sem=r1_sem.at[dl - 1, part],
                    device_id=to,
                    device_id_type=MESH,
                )
            )
    for c in joins:
        c.start()
    for c in joins:
        c.wait_recv()
    parts = [(acc[l], ml[l])] + [(got[n, 0], got[n, 1]) for n in range(NL - 1)]
    top = functools.reduce(jnp.maximum, [p[1][:, :1] for p in parts])
    total = sum(p[1][:, 64:65] * jnp.exp(p[1][:, :1] - top) for p in parts)
    weighted = sum(p[0] * jnp.exp(p[1][:, :1] - top) for p in parts)
    joined = (weighted / total).astype(jnp.bfloat16)
    mine = i * NL + l
    for h in range(16):
        ctx[mine, :, h * 128 : (h + 1) * 128] = joined[h * 16 : (h + 1) * 16, :]

    spread = []
    for di in range(NI):
        for dl in range(NL):
            if di or dl:
                spread.append(
                    pltpu.make_async_remote_copy(
                        src_ref=ctx.at[mine],
                        dst_ref=ctx.at[mine],
                        send_sem=s2_sem.at[di, dl],
                        recv_sem=r2_sem.at[di, dl],
                        device_id=column(di, dl),
                        device_id_type=MESH,
                    )
                )
    for c in spread:
        c.start()
    w_copy.wait()
    for c in spread:
        c.wait_recv()
    context = jnp.dot(order[...], ctx[...].reshape(256, 2048), preferred_element_type=jnp.float32)
    context = context.astype(jnp.bfloat16)
    for n in range(NT):
        proj[n] = jnp.dot(context, w[:, n * 128 : (n + 1) * 128], preferred_element_type=jnp.float32)
    sums = []
    for dt in range(1, NT):
        to = plane(0, dt)
        sums.append(
            pltpu.make_async_remote_copy(
                src_ref=proj.at[to[2]],
                dst_ref=red.at[dt - 1],
                send_sem=s4_sem.at[dt - 1],
                recv_sem=r4_sem.at[dt - 1],
                device_id=to,
                device_id_type=MESH,
            )
        )
    for c in sums:
        c.start()

    total = proj[t] + residual[...].astype(jnp.float32)
    for n, c in enumerate(sums):
        c.wait_recv()
        total = total + red[n]
    attn[...] = total

    zero_out = pltpu.make_async_copy(zero, pages.at[NI * NEAR + FAR], own_sem.at[0])
    zero_out.start()
    zero_out.wait()
    ext_out.wait()
    for c in joins + spread + sums:
        c.wait_send()

    def drain(k, c):
        def one(n, c):
            di, dt = pair(n)

            @pl.when(n != 0)
            def _():
                page_copy(k, di, dt).wait_send()

            return c

        for d in range(NI):
            pltpu.make_async_copy(recv.at[d, k], pages.at[d * NEAR + k], page_sem.at[d, k]).wait()
        return lax.fori_loop(0, NI * NT, one, c)

    lax.fori_loop(0, NEAR, drain, 0)


def run_main(*args):
    hbm, vmem = pl.BlockSpec(memory_space=pl.ANY), pl.BlockSpec(memory_space=pltpu.VMEM)
    bf, f32, dma = jnp.bfloat16, jnp.float32, pltpu.SemaphoreType.DMA
    return pl.pallas_call(
        main_kernel,
        out_shape=(
            jax.ShapeDtypeStruct((NI * NEAR + FAR + 1, NT, 2, 64, 128), bf),
            jax.ShapeDtypeStruct((256, 128), f32),
        ),
        in_specs=[hbm] * 3 + [vmem] * 9,
        out_specs=(hbm, vmem),
        scratch_shapes=[
            pltpu.VMEM((NI, NEAR, NT, 2, 64, 128), bf),
            pltpu.VMEM((FAR, NT, 2, 64, 128), bf),
            pltpu.VMEM((2048, 1024), bf),
            pltpu.VMEM((NI, 256, 128), bf),
            pltpu.VMEM((256, 128), bf),
            pltpu.VMEM((64, 256), bf),
            pltpu.VMEM((NI, 256, 128), f32),
            pltpu.VMEM((NI, 256, 128), f32),
            pltpu.VMEM((NL - 1, 2, 256, 128), f32),
            pltpu.VMEM((NI * NL, 16, 2048), bf),
            pltpu.VMEM((NT, 256, 128), f32),
            pltpu.VMEM((NT - 1, 256, 128), f32),
            pltpu.VMEM((NT, 2, 64, 128), bf),
            dma((NI, NEAR, NT)),
            dma((NI, NEAR, NT)),
            dma((NEAR,)),
            dma((NI, NEAR)),
            dma,
            dma,
            dma((NL - 1, 2)),
            dma((NL - 1, 2)),
            dma((NI, NL)),
            dma((NI, NL)),
            dma((NT - 1,)),
            dma((NT - 1,)),
        ],
        compiler_params=pltpu.CompilerParams(
            collective_id=0, has_side_effects=True, vmem_limit_bytes=48 * 1024 * 1024
        ),
    )(*args)


def shards(
    prefill_pool,
    lengths,
    src_table,
    dst_table,
    row_request,
    positions,
    queries,
    step_key_value,
    out_weight,
    residual,
):
    inst, lay, ten = (lax.axis_index(a) for a in ("instance", "layout", "tensor"))
    src_dev = prefill_pool.shape[0]
    slots = 288
    npages = (lengths + 63) // 64
    src_grp = src_table[:, 0] // (src_dev * NL * NT)
    dec_grp = dst_table[:, 0] // (slots * NL)
    place = jnp.arange(4, dtype=jnp.int32)
    k16 = jnp.arange(16, dtype=jnp.int32)

    rank = (inst * NL + lay) * NT + ten
    own_src = lax.dynamic_slice(src_table.reshape(16, 16, NT, NL), (0, 0, ten, lay), (16, 16, 1, 1)).reshape(16, 16)
    own_src = jnp.clip(own_src - rank * src_dev, 0, src_dev - 1)
    to_place = (src_grp[None, :] == inst) & ((dec_grp[None, :] - inst) % NI == place[:, None])
    slot = jnp.sum(jnp.where(to_place[:, :, None], own_src[None], 0), axis=1)
    longest = lengths == jnp.max(lengths)
    long_slot = jnp.sum(jnp.where(longest[:, None], own_src, 0), axis=0)
    long_src = jnp.sum(jnp.where(longest, src_grp, 0))
    long_dec = jnp.sum(jnp.where(longest, dec_grp, 0))
    send_extra = prefill_pool[long_slot[NEAR:]]
    send = prefill_pool[slot[:, :NEAR]]
    extra = lax.switch(
        long_src * NI + long_dec,
        [functools.partial(move_extra, p, g) for p in range(NI) for g in range(NI)],
        send_extra,
    )

    row_src = jnp.sum(jnp.where(row_request[:, None] == k16[None, :], src_grp[None, :], 0), axis=1)
    rows = jnp.arange(64, dtype=jnp.int32)
    row_grp = rows // 16
    row_place = (row_grp - row_src) % NI
    earlier = (row_request[:, None] == row_request[None, :]) & (rows[None, :] < rows[:, None])
    row_rank = jnp.sum(earlier.astype(jnp.int32), axis=1)
    step = jnp.arange(4, dtype=jnp.int32)
    flat = (row_grp * 64 + row_place * 16 + row_rank)[None, :] + step[:, None] * 4
    order = (flat.reshape(256, 1) == jnp.arange(256, dtype=jnp.int32)[None, :]).astype(jnp.bfloat16)
    local = lax.dynamic_slice_in_dim(row_place * 16 + row_rank, inst * 16, 16)
    local = local[None, :] + step[:, None] * 4
    pick = (jnp.arange(64, dtype=jnp.int32)[:, None] == local.reshape(1, 64)).astype(jnp.bfloat16)
    local_pos = lax.dynamic_slice_in_dim(positions, inst * 16, 16)
    local_place = lax.dynamic_slice_in_dim(row_place, inst * 16, 16)
    local_rank = lax.dynamic_slice_in_dim(row_rank, inst * 16, 16)
    hit = (local_place[None, None, :] == place[:, None, None]) & (local_rank[None, None, :] == place[None, :, None])
    pos = jnp.sum(jnp.where(hit, local_pos[None, None, :], 0), axis=2)
    pos = jnp.broadcast_to(pos[:, None, :], (4, 64, 4)).reshape(4, 256, 1)
    here = (long_dec == inst) & ((inst - long_src) % NI == place)
    pos_x = jnp.sum(jnp.where(here[:, None, None], pos, 0), axis=0)
    pick_x = jnp.sum(jnp.where(here[:, None, None], pick.reshape(4, 16, 64), 0), axis=0).astype(jnp.bfloat16)
    far = jnp.broadcast_to(jnp.where(here, 0.0, 2 * LOW)[:, None], (4, 128)).astype(jnp.float32)

    pages, attn = run_main(
        send,
        extra,
        out_weight,
        queries.reshape(64, 2048),
        step_key_value.reshape(64, 256),
        pick,
        order,
        pos,
        pos_x,
        pick_x,
        far,
        residual.reshape(256, 128),
    )

    own_dst = lax.dynamic_slice_in_dim(dst_table.reshape(16, 16, NT, NL), lay, 1, 3).reshape(16, 16, NT)
    from_place = (dec_grp[None, :] == inst) & ((inst - src_grp[None, :]) % NI == place[:, None])
    target = jnp.sum(jnp.where(from_place[:, :, None, None], own_dst[None], 0), axis=1)
    target = target - (inst * NL + lay) * slots
    count = jnp.sum(jnp.where(from_place, npages[None, :], 0), axis=1)
    t8 = jnp.arange(NT, dtype=jnp.int32)
    page = (k16[:, None] * NT + t8[None, :]) * NL + lay
    live = page[None] < count[:, None, None]
    dt = (ten - t8) % NT
    near = (place[:, None, None] * NEAR + k16[None, :, None]) * NT + dt[None, None, :]
    beyond = (NI * NEAR + k16[None, :, None] - NEAR) * NT + dt[None, None, :]
    source = jnp.where(k16[None, :, None] < NEAR, near, beyond)
    source = jnp.where(live, source, -1).reshape(1, 512)
    match = target.reshape(1, 512) == jnp.arange(slots, dtype=jnp.int32)[:, None]
    index = jnp.max(jnp.where(match, source, -1), axis=1)
    index = jnp.where(index < 0, (NI * NEAR + FAR) * NT, index)
    pool = pages.reshape((NI * NEAR + FAR + 1) * NT, 2, 64, 128)[index]
    return pool.reshape(slots, 2, 1, 64, 128), attn.reshape(4, 64, 128)


def solution(mesh):
    in_specs = (
        P(("instance", "layout", "tensor"), None, None, None, None),
        P(),
        P(),
        P(),
        P(),
        P(),
        P(None, "instance", "tensor"),
        P(None, "instance", None, "tensor", None),
        P("tensor", ("instance", "layout")),
        P(None, None, ("instance", "layout", "tensor")),
    )
    out_specs = (
        P(("instance", "layout"), None, "tensor", None, None),
        P(None, None, ("instance", "layout", "tensor")),
    )
    return jax.shard_map(shards, mesh=mesh, in_specs=in_specs, out_specs=out_specs, check_vma=False)
```

```python
import functools

import jax
import jax.numpy as jnp
from jax import lax
from jax.experimental import pallas as pl
from jax.experimental.pallas import tpu as pltpu
from jax.sharding import PartitionSpec as P

MESH = pl.DeviceIdType.MESH
LOW = -1e30
MASKED = -2e30
NI, NL, NT = 4, 4, 8
NEAR = 6
FAR = 10
LONGEST = 32768
SRC = 36
SLOTS = 288
GROUP = 1152


def routes(p, g):
    way = (g - p) % NI
    if way == 0:
        return [(0, FAR, [])]
    if way == 2:
        return [(0, FAR // 2, [(p + 1) % NI]), (FAR // 2, FAR, [(p - 1) % NI])]
    return [(0, 6, []), (6, FAR, [(p - way) % NI, (p - 2 * way) % NI])]


def find(lengths):
    return functools.reduce(lambda best, r: jnp.where(lengths[r] == LONGEST, r, best), range(16), jnp.int32(0))


def extra_kernel(p, g, lengths, table, pool, dst, held, packed, hop, zero, send_sem, recv_sem, hop_send, hop_recv, fill_sem):
    i, l, t = (lax.axis_index(a) for a in ("instance", "layout", "tensor"))
    barrier = pltpu.get_barrier_semaphore()

    def hop_copy(k, half, src, to):
        return pltpu.make_async_remote_copy(
            src_ref=src,
            dst_ref=hop.at[k, half],
            send_sem=hop_send.at[k, half],
            recv_sem=hop_recv.at[k, half],
            device_id=(to, l, t),
            device_id_type=MESH,
        )

    def last_copy(k, head, src):
        dt = lax.rem(head - t + NT, NT)
        return pltpu.make_async_remote_copy(
            src_ref=src,
            dst_ref=dst.at[k, dt],
            send_sem=send_sem.at[dt, k],
            recv_sem=recv_sem.at[dt, k],
            device_id=(g, l, head),
            device_id_type=MESH,
        )

    first = 1 if p == g else 0

    for lo, hi, via in routes(p, g):
        nodes = [p] + via

        @pl.when(i == g)
        def _():
            for dt in range(first, NT):
                to = (nodes[-1], l, lax.rem(t + dt, NT))
                pl.semaphore_signal(barrier, inc=1, device_id=to, device_id_type=MESH)

        for before, after in zip(nodes, via):

            @pl.when(i == after)
            def _():
                pl.semaphore_signal(barrier, inc=1, device_id=(before, l, t), device_id_type=MESH)

    @pl.when(i == p)
    def _():
        load = pltpu.make_async_copy(pool, held, fill_sem.at[0])
        load.start()
        pl.semaphore_wait(barrier, sum(1 if via else NT - first for _, _, via in routes(p, g)))
        load.wait()
        request = find(lengths)
        rank = (i * NL + l) * NT + t

        def pack(k):
            slot = table[request, ((NEAR + k) * NT + t) * NL + l] - rank * SRC
            packed[k] = held[jnp.clip(slot, 0, SRC - 1)]

        def direct(k, c):
            pack(k)
            for dt in range(first, NT):
                head = lax.rem(t + dt, NT)
                last_copy(k, head, packed.at[k, :, head]).start()
            return c

        def relayed(to, k, c):
            pack(k)
            for half in range(2):
                hop_copy(k, half, packed.at[k, :, half * 4 : half * 4 + 4], to).start()
            return c

        for lo, hi, via in reversed(routes(p, g)):
            lax.fori_loop(lo, hi, functools.partial(relayed, via[0]) if via else direct, 0)

    for lo, hi, via in routes(p, g):
        for n, node in enumerate(via):

            @pl.when(i == node)
            def _():
                pl.semaphore_wait(barrier, 1 if n + 1 < len(via) else NT)

                def forward(k, c):
                    for half in range(2):
                        hop_copy(k, half, hop.at[k, half], node).wait_recv()
                        if n + 1 < len(via):
                            hop_copy(k, half, hop.at[k, half], via[n + 1]).start()
                        else:
                            for hh in range(4):
                                h = lax.rem(t + hh, 4)
                                last_copy(k, half * 4 + h, hop.at[k, half, :, h]).start()
                    return c

                lax.fori_loop(lo, hi, forward, 0)

    if p == g:

        @pl.when(i == g)
        def _():
            own = pltpu.make_async_copy(packed.at[:, :, t], dst.at[:, 0], fill_sem.at[0])
            own.start()
            own.wait()

    @pl.when(i != g)
    def _():
        zero[...] = jnp.zeros_like(zero)
        fills = [pltpu.make_async_copy(zero, dst.at[k], fill_sem.at[k]) for k in range(FAR)]
        for f in fills:
            f.start()
        for f in fills:
            f.wait()

    for lo, hi, via in routes(p, g):
        nodes = [p] + via
        for n, node in enumerate(nodes):

            @pl.when(i == node)
            def _():
                def drain(k, c):
                    if n + 1 < len(nodes):
                        for half in range(2):
                            hop_copy(k, half, hop.at[k, half], node).wait_send()
                    else:
                        for dt in range(first, NT):
                            head = lax.rem(t + dt, NT)
                            last_copy(k, head, packed.at[k, :, head]).wait_send()
                    return c

                lax.fori_loop(lo, hi, drain, 0)

    @pl.when(i == g)
    def _():
        def arrive(k, c):
            for dt in range(first, NT):
                head = lax.rem(t + dt, NT)
                last_copy(k, head, packed.at[k, :, head]).wait_recv()
            return c

        lax.fori_loop(0, FAR, arrive, 0)


def move_extra(p, g, lengths, table, pool):
    smem, hbm = pl.BlockSpec(memory_space=pltpu.SMEM), pl.BlockSpec(memory_space=pl.ANY)
    bf, dma = jnp.bfloat16, pltpu.SemaphoreType.DMA
    return pl.pallas_call(
        functools.partial(extra_kernel, p, g),
        out_shape=jax.ShapeDtypeStruct((FAR, NT, 2, 64, 128), bf),
        in_specs=[smem, smem, hbm],
        out_specs=hbm,
        scratch_shapes=[
            pltpu.VMEM((SRC, 2, NT, 64, 128), bf),
            pltpu.VMEM((FAR, 2, NT, 64, 128), bf),
            pltpu.VMEM((FAR, 2, 2, 4, 64, 128), bf),
            pltpu.VMEM((NT, 2, 64, 128), bf),
            dma((NT, FAR)),
            dma((NT, FAR)),
            dma((FAR, 2)),
            dma((FAR, 2)),
            dma((FAR,)),
        ],
        compiler_params=pltpu.CompilerParams(
            collective_id=1 + p * NI + g, has_side_effects=True, vmem_limit_bytes=32 * 1024 * 1024
        ),
    )(lengths, table, pool)


def main_kernel(
    table,
    target,
    lengths,
    row_request,
    positions,
    pool,
    extra,
    weight,
    target_v,
    query,
    fresh,
    residual,
    pages,
    attn,
    index,
    held,
    send,
    recv,
    ext,
    w,
    q,
    qx,
    fkv,
    pos,
    acc,
    ml,
    got,
    ctx,
    proj,
    red,
    zero,
    send_sem,
    recv_sem,
    own_sem,
    page_sem,
    w_sem,
    ext_sem,
    pool_sem,
    s1_sem,
    r1_sem,
    s2_sem,
    r2_sem,
    s4_sem,
    r4_sem,
):
    i, l, t = (lax.axis_index(a) for a in ("instance", "layout", "tensor"))
    scale = 128.0**-0.5

    def plane(di, dt):
        return (lax.rem(i + di, NI), l, lax.rem(t + dt, NT))

    def column(di, dl):
        return (lax.rem(i + di, NI), lax.rem(l + dl, NL), t)

    barrier = pltpu.get_barrier_semaphore()
    load = pltpu.make_async_copy(pool, held, pool_sem)
    load.start()
    for di in range(NI):
        for dt in range(NT):
            if di or dt:
                pl.semaphore_signal(barrier, inc=1, device_id=plane(di, dt), device_id_type=MESH)
    for di in range(NI):
        for dl in range(1, NL):
            pl.semaphore_signal(barrier, inc=1, device_id=column(di, dl), device_id_type=MESH)

    w_copy = pltpu.make_async_copy(weight, w, w_sem)
    ext_copy = pltpu.make_async_copy(extra, ext, ext_sem)
    ext_copy.start()
    own = [pltpu.make_async_copy(send.at[0, k, :, t], recv.at[0, k, 0], own_sem.at[k]) for k in range(NEAR)]

    out_req = [jnp.int32(0)] * NI
    in_req = [jnp.int32(0)] * NI
    for r in range(16):
        src_r, dst_r = lax.div(table[r, 0], GROUP), lax.div(target[r, 0], GROUP)
        for d in range(NI):
            out_req[d] = jnp.where((src_r == i) & (dst_r == lax.rem(i + d, NI)), r, out_req[d])
            in_req[d] = jnp.where((dst_r == i) & (src_r == lax.rem(i + NI - d, NI)), r, in_req[d])
    rank = (i * NL + l) * NT + t
    pl.semaphore_wait(barrier, NI * NT - 1 + NI * (NL - 1))
    load.wait()

    def page_copy(k, di, dt):
        to = plane(di, dt)
        return pltpu.make_async_remote_copy(
            src_ref=send.at[di, k, :, to[2]],
            dst_ref=recv.at[di, k, dt],
            send_sem=send_sem.at[di, k, dt],
            recv_sem=recv_sem.at[di, k, dt],
            device_id=to,
            device_id_type=MESH,
        )

    def pair(n):
        di = n % 4
        dz = (di + n // 8) % 4
        return di, dz * 2 + (n // 4) % 2

    def send_page(k, c):
        for d in range(NI):
            slot = table[out_req[d], (k * NT + t) * NL + l] - rank * SRC
            send[d, k] = held[jnp.clip(slot, 0, SRC - 1)]

        def one(n, c):
            di, dt = pair(n)

            @pl.when(n != 0)
            def _():
                page_copy(k, di, dt).start()

            return c

        return lax.fori_loop(0, NI * NT, one, c)

    lax.fori_loop(0, NEAR, send_page, 0)
    w_copy.start()

    for c in own:
        c.start()

    def places(group):
        count, found = [jnp.int32(0)] * NI, []
        for n in range(16):
            request = row_request[group * 16 + n]
            d = lax.rem(group - lax.div(table[request, 0], GROUP) + NI, NI)
            rank = functools.reduce(lambda x, m: jnp.where(d == m, count[m], x), range(1, NI), count[0])
            count = [jnp.where(d == m, count[m] + 1, count[m]) for m in range(NI)]
            found.append((d, rank))
        return found

    def one_hot(found, by, plain):
        step = plain // 16
        hit = functools.reduce(
            jnp.logical_or, [(plain % 16 == n) & (by - step * 4 == d * 16 + rank) for n, (d, rank) in enumerate(found)]
        )
        return jnp.where(hit, 1.0, 0.0).astype(jnp.bfloat16)

    down = lax.broadcasted_iota(jnp.int32, (64, 64), 0)
    across = lax.broadcasted_iota(jnp.int32, (64, 64), 1)
    here = places(i)
    pick = one_hot(here, down, across)

    sorted_q = jnp.dot(pick, query[...], preferred_element_type=jnp.float32).astype(jnp.bfloat16)
    fkv[...] = jnp.dot(pick, fresh[...], preferred_element_type=jnp.float32).astype(jnp.bfloat16)
    for h in range(16):
        for d in range(NI):
            q[d, h * 16 : (h + 1) * 16, :] = sorted_q[d * 16 : (d + 1) * 16, h * 128 : (h + 1) * 128]
    in_row = lax.broadcasted_iota(jnp.int32, (256, 128), 0) % 4
    flag = [jnp.where(lengths[in_req[d]] == LONGEST, 1, 0) for d in range(NI)]
    qx[...] = jnp.zeros_like(qx)
    pos[NI] = jnp.zeros((256, 128), jnp.int32)
    for d in range(NI):
        seen = [jnp.int32(0)] * 4
        for n, (place, rank) in enumerate(here):
            seen = [jnp.where((place == d) & (rank == m), positions[i * 16 + n], seen[m]) for m in range(4)]
        pos[d] = functools.reduce(lambda x, m: jnp.where(in_row == m, seen[m], x), range(1, 4), jnp.full((256, 128), seen[0]))
        pos[NI] += pos[d] * flag[d]
        qx[...] = jnp.where(jnp.full((256, 128), flag[d]) == 1, q[d].astype(jnp.float32), qx[...])

    slot_of = lax.broadcasted_iota(jnp.int32, (384, 512), 0)
    j = lax.broadcasted_iota(jnp.int32, (1, 512), 1)
    k, dt = j // 32, (t - j // 4 + 2 * 512) % NT
    found = jnp.full((384, 512), -1, jnp.int32)
    for d in range(NI):
        page = jnp.where(k < NEAR, (d * NEAR + k) * NT + dt, (NI * NEAR + k - NEAR) * NT + dt)
        goes = (j % NL == l) & (j * 64 < lengths[in_req[d]])
        to = jnp.where(goes, target_v[pl.ds(in_req[d], 1), :] - (i * NL + l) * SLOTS, -1)
        found = jnp.where(slot_of == to, page, found)
    found = jnp.max(found, axis=1, keepdims=True)
    found = jnp.where(found < 0, (NI * NEAR + FAR) * NT, found)
    eye = lax.broadcasted_iota(jnp.int32, (128, 128), 0) == lax.broadcasted_iota(jnp.int32, (128, 128), 1)
    for n in range(3):
        column_n = jnp.broadcast_to(found[n * 128 : (n + 1) * 128], (128, 128))
        index[n : n + 1, :] = jnp.sum(jnp.where(eye, column_n, 0), axis=0, keepdims=True)
    zero[...] = jnp.zeros_like(zero)

    def update(m, total, weighted, s, v):
        top = jnp.maximum(m, jnp.max(s, axis=1, keepdims=True))
        shrink = jnp.exp(m - top)
        p = jnp.exp(s - top)
        total = total * shrink + jnp.sum(p, axis=1, keepdims=True)
        weighted = weighted * shrink + jnp.dot(p.astype(jnp.bfloat16), v, preferred_element_type=jnp.float32)
        return top, total, weighted

    def dots(a, b):
        return lax.dot_general(a, b, (((1,), (1,)), ((), ())), preferred_element_type=jnp.float32) * scale

    ext_copy.wait()
    ext_out = pltpu.make_async_copy(ext, pages.at[pl.ds(NI * NEAR, FAR)], ext_sem)
    ext_out.start()

    def extra_step(k, carry):
        n = lax.broadcasted_iota(jnp.int32, (1, NT * 64), 1)
        ts = (t + NT - n // 64) % NT
        token = (((NEAR + k) * NT + ts) * NL + l) * 64 + n % 64
        s = dots(qx[...].astype(jnp.bfloat16), ext[k, :, 0].reshape(NT * 64, 128))
        s = jnp.where(token < pos[NI, :, :1], s, MASKED)
        return update(*carry, s, ext[k, :, 1].reshape(NT * 64, 128))

    empty = (
        jnp.full((256, 1), LOW, jnp.float32),
        jnp.zeros((256, 1), jnp.float32),
        jnp.zeros((256, 128), jnp.float32),
    )
    mx, tx, ax = lax.fori_loop(0, FAR, extra_step, empty)

    a = lax.broadcasted_iota(jnp.int32, (256, 16), 0)
    b = lax.broadcasted_iota(jnp.int32, (256, 16), 1)
    visible = (a % 4 == b % 4) & (b // 4 <= (a // 4) % 4) & (l == 0)
    for d in range(NI):
        rows = slice(d * 16, (d + 1) * 16)
        s = jnp.where(visible, dots(q[d], fkv[rows, :128]), MASKED)
        far = jnp.full((256, 1), flag[d]) == 1
        start = (jnp.where(far, mx, LOW), jnp.where(far, tx, 0.0), jnp.where(far, ax, 0.0))
        m, total, weighted = update(*start, s, fkv[rows, 128:])
        acc[d] = weighted
        ml[d, :, :64] = jnp.broadcast_to(m, (256, 64))
        ml[d, :, 64:] = jnp.broadcast_to(total, (256, 64))

    for c in own:
        c.wait()

    def visit(k, c):
        def request(d, c):
            for dt in range(NT):
                if dt:
                    page_copy(k, d, dt).wait_recv()
                else:

                    @pl.when(d != 0)
                    def _():
                        page_copy(k, d, dt).wait_recv()

            pltpu.make_async_copy(recv.at[d, k], pages.at[d * NEAR + k], page_sem.at[d, k]).start()
            n = lax.broadcasted_iota(jnp.int32, (1, NT * 64), 1)
            ts = (t + NT - n // 64) % NT
            token = ((k * NT + ts) * NL + l) * 64 + n % 64
            s = dots(q[d], recv[d, k, :, 0].reshape(NT * 64, 128))
            s = jnp.where(token < pos[d, :, :1], s, MASKED)
            m, total, weighted = update(
                ml[d, :, :1], ml[d, :, 64:65], acc[d], s, recv[d, k, :, 1].reshape(NT * 64, 128)
            )
            acc[d] = weighted
            ml[d, :, :64] = jnp.broadcast_to(m, (256, 64))
            ml[d, :, 64:] = jnp.broadcast_to(total, (256, 64))
            return c

        return lax.fori_loop(0, NI, request, c)

    lax.fori_loop(0, NEAR, visit, 0)

    joins = []
    for dl in range(1, NL):
        to = column(0, dl)
        for part, ref in enumerate((acc, ml)):
            joins.append(
                pltpu.make_async_remote_copy(
                    src_ref=ref.at[to[1]],
                    dst_ref=got.at[dl - 1, part],
                    send_sem=s1_sem.at[dl - 1, part],
                    recv_sem=r1_sem.at[dl - 1, part],
                    device_id=to,
                    device_id_type=MESH,
                )
            )
    for c in joins:
        c.start()
    for c in joins:
        c.wait_recv()
    parts = [(acc[l], ml[l])] + [(got[n, 0], got[n, 1]) for n in range(NL - 1)]
    top = functools.reduce(jnp.maximum, [p[1][:, :1] for p in parts])
    total = sum(p[1][:, 64:65] * jnp.exp(p[1][:, :1] - top) for p in parts)
    weighted = sum(p[0] * jnp.exp(p[1][:, :1] - top) for p in parts)
    joined = (weighted / total).astype(jnp.bfloat16)
    mine = i * NL + l
    for h in range(16):
        ctx[mine, :, h * 128 : (h + 1) * 128] = joined[h * 16 : (h + 1) * 16, :]

    spread = []
    for di in range(NI):
        for dl in range(NL):
            if di or dl:
                spread.append(
                    pltpu.make_async_remote_copy(
                        src_ref=ctx.at[mine],
                        dst_ref=ctx.at[mine],
                        send_sem=s2_sem.at[di, dl],
                        recv_sem=r2_sem.at[di, dl],
                        device_id=column(di, dl),
                        device_id_type=MESH,
                    )
                )
    for c in spread:
        c.start()
    w_copy.wait()
    for c in spread:
        c.wait_recv()
    context = []
    for group in range(NI):
        back = one_hot(places(jnp.int32(group)), across, down)
        rows = ctx[group * NL : (group + 1) * NL].reshape(64, 2048)
        context.append(jnp.dot(back, rows, preferred_element_type=jnp.float32).astype(jnp.bfloat16))
    context = jnp.concatenate(context, axis=0)
    for n in range(NT):
        proj[n] = jnp.dot(context, w[:, n * 128 : (n + 1) * 128], preferred_element_type=jnp.float32)
    sums = []
    for dt in range(1, NT):
        to = plane(0, dt)
        sums.append(
            pltpu.make_async_remote_copy(
                src_ref=proj.at[to[2]],
                dst_ref=red.at[dt - 1],
                send_sem=s4_sem.at[dt - 1],
                recv_sem=r4_sem.at[dt - 1],
                device_id=to,
                device_id_type=MESH,
            )
        )
    for c in sums:
        c.start()

    total = proj[t]
    for n, c in enumerate(sums):
        c.wait_recv()
        total = total + red[n]
    for group in range(NI):
        mine = slice(group * 16, (group + 1) * 16)
        for step in range(4):
            rows = total[group * 64 + step * 16 : group * 64 + (step + 1) * 16]
            attn[step, mine] = rows + residual[step, mine].astype(jnp.float32)

    zero_out = pltpu.make_async_copy(zero, pages.at[NI * NEAR + FAR], own_sem.at[0])
    zero_out.start()
    zero_out.wait()
    ext_out.wait()
    for c in joins + spread + sums:
        c.wait_send()

    def drain(k, c):
        def one(n, c):
            di, dt = pair(n)

            @pl.when(n != 0)
            def _():
                page_copy(k, di, dt).wait_send()

            return c

        for d in range(NI):
            pltpu.make_async_copy(recv.at[d, k], pages.at[d * NEAR + k], page_sem.at[d, k]).wait()
        return lax.fori_loop(0, NI * NT, one, c)

    lax.fori_loop(0, NEAR, drain, 0)


def run_main(*args):
    hbm, vmem, smem = (pl.BlockSpec(memory_space=m) for m in (pl.ANY, pltpu.VMEM, pltpu.SMEM))
    bf, f32, i32, dma = jnp.bfloat16, jnp.float32, jnp.int32, pltpu.SemaphoreType.DMA
    return pl.pallas_call(
        main_kernel,
        out_shape=(
            jax.ShapeDtypeStruct((NI * NEAR + FAR + 1, NT, 2, 64, 128), bf),
            jax.ShapeDtypeStruct((4, 64, 128), f32),
            jax.ShapeDtypeStruct((3, 128), i32),
        ),
        in_specs=[smem] * 5 + [hbm] * 3 + [vmem] * 4,
        out_specs=(hbm, vmem, vmem),
        scratch_shapes=[
            pltpu.VMEM((SRC, 2, NT, 64, 128), bf),
            pltpu.VMEM((NI, NEAR, 2, NT, 64, 128), bf),
            pltpu.VMEM((NI, NEAR, NT, 2, 64, 128), bf),
            pltpu.VMEM((FAR, NT, 2, 64, 128), bf),
            pltpu.VMEM((2048, 1024), bf),
            pltpu.VMEM((NI, 256, 128), bf),
            pltpu.VMEM((256, 128), f32),
            pltpu.VMEM((64, 256), bf),
            pltpu.VMEM((NI + 1, 256, 128), i32),
            pltpu.VMEM((NI, 256, 128), f32),
            pltpu.VMEM((NI, 256, 128), f32),
            pltpu.VMEM((NL - 1, 2, 256, 128), f32),
            pltpu.VMEM((NI * NL, 16, 2048), bf),
            pltpu.VMEM((NT, 256, 128), f32),
            pltpu.VMEM((NT - 1, 256, 128), f32),
            pltpu.VMEM((NT, 2, 64, 128), bf),
            dma((NI, NEAR, NT)),
            dma((NI, NEAR, NT)),
            dma((NEAR,)),
            dma((NI, NEAR)),
            dma,
            dma,
            dma,
            dma((NL - 1, 2)),
            dma((NL - 1, 2)),
            dma((NI, NL)),
            dma((NI, NL)),
            dma((NT - 1,)),
            dma((NT - 1,)),
        ],
        compiler_params=pltpu.CompilerParams(
            collective_id=0, has_side_effects=True, vmem_limit_bytes=56 * 1024 * 1024
        ),
    )(*args)


def place_kernel(index, pages, pool, held, load_sem, sem):
    load = pltpu.make_async_copy(pages, held, load_sem)
    load.start()
    load.wait()

    def place(s, c):
        pltpu.make_async_copy(held.at[index[s // 128, s % 128]], pool.at[s], sem).start()
        return c

    lax.fori_loop(0, SLOTS, place, 0, unroll=8)
    pltpu.make_async_copy(pool, pool, sem).wait()


def place_pages(index, pages):
    smem, hbm = pl.BlockSpec(memory_space=pltpu.SMEM), pl.BlockSpec(memory_space=pl.ANY)
    return pl.pallas_call(
        place_kernel,
        out_shape=jax.ShapeDtypeStruct((SLOTS, 2, 64, 128), jnp.bfloat16),
        in_specs=[smem, hbm],
        out_specs=hbm,
        scratch_shapes=[
            pltpu.VMEM(pages.shape, jnp.bfloat16),
            pltpu.SemaphoreType.DMA,
            pltpu.SemaphoreType.DMA,
        ],
        compiler_params=pltpu.CompilerParams(vmem_limit_bytes=16 * 1024 * 1024),
    )(index, pages)


def shards(
    prefill_pool,
    lengths,
    src_table,
    dst_table,
    row_request,
    positions,
    queries,
    step_key_value,
    out_weight,
    residual,
):
    route = src_table[:, 0] // GROUP * NI + dst_table[:, 0] // GROUP
    extra = lax.switch(
        jnp.sum(jnp.where(lengths == LONGEST, route, 0)),
        [functools.partial(move_extra, p, g) for p in range(NI) for g in range(NI)],
        lengths,
        src_table,
        prefill_pool,
    )
    pages, attn, index = run_main(
        src_table,
        dst_table,
        lengths,
        row_request,
        positions,
        prefill_pool,
        extra,
        out_weight,
        dst_table,
        queries.reshape(64, 2048),
        step_key_value.reshape(64, 256),
        residual,
    )
    pool = place_pages(index, pages.reshape((NI * NEAR + FAR + 1) * NT, 2, 64, 128))
    return pool.reshape(SLOTS, 2, 1, 64, 128), attn


def solution(mesh):
    in_specs = (
        P(("instance", "layout", "tensor"), None, None, None, None),
        P(),
        P(),
        P(),
        P(),
        P(),
        P(None, "instance", "tensor"),
        P(None, "instance", None, "tensor", None),
        P("tensor", ("instance", "layout")),
        P(None, None, ("instance", "layout", "tensor")),
    )
    out_specs = (
        P(("instance", "layout"), None, "tensor", None, None),
        P(None, None, ("instance", "layout", "tensor")),
    )
    return jax.shard_map(shards, mesh=mesh, in_specs=in_specs, out_specs=out_specs, check_vma=False)
```

```python
import functools

import jax
import jax.numpy as jnp
from jax import lax
from jax.experimental import pallas as pl
from jax.experimental.pallas import tpu as pltpu
from jax.sharding import PartitionSpec as P

MESH = pl.DeviceIdType.MESH
LOW = -1e30
MASKED = -2e30
NI, NL, NT = 4, 4, 8
NEAR = 6
PARTS = 4
HEADS = NT // PARTS
AHEAD = 3
FAR = 10
LONGEST = 32768
SRC = 36
SLOTS = 288
GROUP = 1152


def routes(p, g):
    way = (g - p) % NI
    if way == 0:
        return [(0, FAR, [])]
    if way == 2:
        return [(0, FAR // 2, [(p + 1) % NI]), (FAR // 2, FAR, [(p - 1) % NI])]
    return [(0, FAR // 2, []), (FAR // 2, FAR, [(p - way) % NI, (p - 2 * way) % NI])]


def find(lengths):
    return functools.reduce(lambda best, r: jnp.where(lengths[r] == LONGEST, r, best), range(16), jnp.int32(0))


def extra_kernel(p, g, lengths, table, pool, dst, held, packed, hop, zero, send_sem, recv_sem, hop_send, hop_recv, fill_sem):
    i, l, t = (lax.axis_index(a) for a in ("instance", "layout", "tensor"))
    barrier = pltpu.get_barrier_semaphore()

    def hop_copy(k, part, src, to):
        return pltpu.make_async_remote_copy(
            src_ref=src,
            dst_ref=hop.at[k, part],
            send_sem=hop_send.at[k, part],
            recv_sem=hop_recv.at[k, part],
            device_id=(to, l, t),
            device_id_type=MESH,
        )

    def last_copy(k, head, src):
        dt = lax.rem(head - t + NT, NT)
        return pltpu.make_async_remote_copy(
            src_ref=src,
            dst_ref=dst.at[k, dt],
            send_sem=send_sem.at[dt, k],
            recv_sem=recv_sem.at[dt, k],
            device_id=(g, l, head),
            device_id_type=MESH,
        )

    first = 1 if p == g else 0

    for lo, hi, via in routes(p, g):
        nodes = [p] + via

        @pl.when(i == g)
        def _():
            for dt in range(first, NT):
                to = (nodes[-1], l, lax.rem(t + dt, NT))
                pl.semaphore_signal(barrier, inc=1, device_id=to, device_id_type=MESH)

        for before, after in zip(nodes, via):

            @pl.when(i == after)
            def _():
                pl.semaphore_signal(barrier, inc=1, device_id=(before, l, t), device_id_type=MESH)

    @pl.when(i == p)
    def _():
        load = pltpu.make_async_copy(pool, held, fill_sem.at[0])
        load.start()
        pl.semaphore_wait(barrier, sum(1 if via else NT - first for _, _, via in routes(p, g)))
        load.wait()
        request = find(lengths)
        rank = (i * NL + l) * NT + t

        def pack(k):
            slot = table[request, ((NEAR + k) * NT + t) * NL + l] - rank * SRC
            packed[k] = held[jnp.clip(slot, 0, SRC - 1)]

        def send(k, c):
            for lo, hi, via in reversed(routes(p, g)):

                @pl.when(lo + k < hi)
                def _():
                    pack(lo + k)
                    if via:
                        for part in range(PARTS):
                            src = packed.at[lo + k, :, part * HEADS : (part + 1) * HEADS]
                            hop_copy(lo + k, part, src, via[0]).start()
                    else:
                        for dt in range(first, NT):
                            head = lax.rem(t + dt, NT)
                            last_copy(lo + k, head, packed.at[lo + k, :, head]).start()

            return c

        lax.fori_loop(0, max(hi - lo for lo, hi, _ in routes(p, g)), send, 0)

    for lo, hi, via in routes(p, g):
        for n, node in enumerate(via):

            @pl.when(i == node)
            def _():
                pl.semaphore_wait(barrier, 1 if n + 1 < len(via) else NT)

                def forward(k, c):
                    for part in range(PARTS):
                        hop_copy(k, part, hop.at[k, part], node).wait_recv()
                        if n + 1 < len(via):
                            hop_copy(k, part, hop.at[k, part], via[n + 1]).start()
                        else:
                            for hh in range(HEADS):
                                h = lax.rem(t + hh, HEADS)
                                last_copy(k, part * HEADS + h, hop.at[k, part, :, h]).start()
                    return c

                lax.fori_loop(lo, hi, forward, 0)

    if p == g:

        @pl.when(i == g)
        def _():
            own = pltpu.make_async_copy(packed.at[:, :, t], dst.at[:, 0], fill_sem.at[0])
            own.start()
            own.wait()

    @pl.when(i != g)
    def _():
        zero[...] = jnp.zeros_like(zero)
        fills = [pltpu.make_async_copy(zero, dst.at[k], fill_sem.at[k]) for k in range(FAR)]
        for f in fills:
            f.start()
        for f in fills:
            f.wait()

    for lo, hi, via in routes(p, g):
        nodes = [p] + via
        for n, node in enumerate(nodes):

            @pl.when(i == node)
            def _():
                def drain(k, c):
                    if n + 1 < len(nodes):
                        for part in range(PARTS):
                            hop_copy(k, part, hop.at[k, part], node).wait_send()
                    else:
                        for dt in range(first, NT):
                            head = lax.rem(t + dt, NT)
                            last_copy(k, head, packed.at[k, :, head]).wait_send()
                    return c

                lax.fori_loop(lo, hi, drain, 0)

    @pl.when(i == g)
    def _():
        def arrive(k, c):
            for dt in range(first, NT):
                head = lax.rem(t + dt, NT)
                last_copy(k, head, packed.at[k, :, head]).wait_recv()
            return c

        lax.fori_loop(0, FAR, arrive, 0)


def move_extra(p, g, lengths, table, pool):
    smem, hbm = pl.BlockSpec(memory_space=pltpu.SMEM), pl.BlockSpec(memory_space=pl.ANY)
    bf, dma = jnp.bfloat16, pltpu.SemaphoreType.DMA
    return pl.pallas_call(
        functools.partial(extra_kernel, p, g),
        out_shape=jax.ShapeDtypeStruct((FAR, NT, 2, 64, 128), bf),
        in_specs=[smem, smem, hbm],
        out_specs=hbm,
        scratch_shapes=[
            pltpu.VMEM((SRC, 2, NT, 64, 128), bf),
            pltpu.VMEM((FAR, 2, NT, 64, 128), bf),
            pltpu.VMEM((FAR, PARTS, 2, HEADS, 64, 128), bf),
            pltpu.VMEM((NT, 2, 64, 128), bf),
            dma((NT, FAR)),
            dma((NT, FAR)),
            dma((FAR, PARTS)),
            dma((FAR, PARTS)),
            dma((FAR,)),
        ],
        compiler_params=pltpu.CompilerParams(
            collective_id=1 + p * NI + g, has_side_effects=True, vmem_limit_bytes=32 * 1024 * 1024
        ),
    )(lengths, table, pool)


def main_kernel(
    table,
    target,
    lengths,
    row_request,
    positions,
    pool,
    extra,
    weight,
    target_v,
    query,
    fresh,
    residual,
    pages,
    attn,
    index,
    held,
    send,
    recv,
    ext,
    w,
    q,
    qx,
    fkv,
    pos,
    acc,
    ml,
    back,
    reqs,
    give,
    got,
    ctx,
    proj,
    red,
    zero,
    send_sem,
    recv_sem,
    own_sem,
    page_sem,
    w_sem,
    ext_sem,
    pool_sem,
    s1_sem,
    r1_sem,
    s2_sem,
    r2_sem,
    s4_sem,
    r4_sem,
):
    i, l, t = (lax.axis_index(a) for a in ("instance", "layout", "tensor"))
    scale = 128.0**-0.5

    def plane(di, dt):
        return (lax.rem(i + di, NI), l, lax.rem(t + dt, NT))

    def column(di, dl):
        return (lax.rem(i + di, NI), lax.rem(l + dl, NL), t)

    barrier = pltpu.get_barrier_semaphore()
    load = pltpu.make_async_copy(pool, held, pool_sem)
    load.start()
    for di in range(NI):
        for dt in range(NT):
            if di or dt:
                pl.semaphore_signal(barrier, inc=1, device_id=plane(di, dt), device_id_type=MESH)
    for di in range(NI):
        for dl in range(1, NL):
            pl.semaphore_signal(barrier, inc=1, device_id=column(di, dl), device_id_type=MESH)

    w_copy = pltpu.make_async_copy(weight, w, w_sem)
    ext_copy = pltpu.make_async_copy(extra, ext, ext_sem)
    ext_copy.start()

    def own_copy(k):
        return pltpu.make_async_copy(send.at[0, k, :, t], recv.at[0, k, 0], own_sem.at[k])

    out_req = [jnp.int32(0)] * NI
    in_req = [jnp.int32(0)] * NI
    for r in range(16):
        src_r, dst_r = lax.div(table[r, 0], GROUP), lax.div(target[r, 0], GROUP)
        for d in range(NI):
            out_req[d] = jnp.where((src_r == i) & (dst_r == lax.rem(i + d, NI)), r, out_req[d])
            in_req[d] = jnp.where((dst_r == i) & (src_r == lax.rem(i + NI - d, NI)), r, in_req[d])
    for d in range(NI):
        reqs[d] = out_req[d]
    base = ((i * NL + l) * NT + t) * SRC
    pl.semaphore_wait(barrier, NI * NT - 1 + NI * (NL - 1))
    load.wait()

    def page_copy(k, di, dt):
        to = plane(di, dt)
        return pltpu.make_async_remote_copy(
            src_ref=send.at[di, k, :, to[2]],
            dst_ref=recv.at[di, k, dt],
            send_sem=send_sem.at[di, k, dt],
            recv_sem=recv_sem.at[di, k, dt],
            device_id=to,
            device_id_type=MESH,
        )

    def pair(n, m):
        d = n // NEAR + 2 * ((m // 2) % 2)
        return d, ((d + m // 4) % 4) * 2 + m % 2

    def each(n, act):
        def one(m, c):
            d, dt = pair(n, m)

            @pl.when((d != 0) | (dt != 0))
            def _():
                act(page_copy(n % NEAR, d, dt))

            return c

        lax.fori_loop(0, 16, one, 0)

    def issue(n, c):
        k = n % NEAR
        for half in range(2):
            d = n // NEAR + 2 * half
            slot = table[reqs[d], (k * NT + t) * NL + l] - base
            send[d, k] = held[jnp.clip(slot, 0, SRC - 1)]
        each(n, lambda c: c.start())

        @pl.when(n < NEAR)
        def _():
            own_copy(k).start()

        return c

    lax.fori_loop(0, AHEAD, issue, 0)
    w_copy.start()

    def places(group):
        count, found = [jnp.int32(0)] * NI, []
        for n in range(16):
            request = row_request[group * 16 + n]
            d = lax.rem(group - lax.div(table[request, 0], GROUP) + NI, NI)
            rank = functools.reduce(lambda x, m: jnp.where(d == m, count[m], x), range(1, NI), count[0])
            count = [jnp.where(d == m, count[m] + 1, count[m]) for m in range(NI)]
            found.append((d, rank))
        return found

    def one_hot(found, by, plain):
        step = plain // 16
        hit = functools.reduce(
            jnp.logical_or, [(plain % 16 == n) & (by - step * 4 == d * 16 + rank) for n, (d, rank) in enumerate(found)]
        )
        return jnp.where(hit, 1.0, 0.0).astype(jnp.bfloat16)

    down = lax.broadcasted_iota(jnp.int32, (64, 64), 0)
    across = lax.broadcasted_iota(jnp.int32, (64, 64), 1)
    here = places(i)
    pick = one_hot(here, down, across)

    for group in range(NI):
        back[group] = one_hot(places(jnp.int32(group)), across, down)

    sorted_q = jnp.dot(pick, query[...], preferred_element_type=jnp.float32).astype(jnp.bfloat16)
    fkv[...] = jnp.dot(pick, fresh[...], preferred_element_type=jnp.float32).astype(jnp.bfloat16)
    for h in range(16):
        for d in range(NI):
            q[d, h * 16 : (h + 1) * 16, :] = sorted_q[d * 16 : (d + 1) * 16, h * 128 : (h + 1) * 128]
    in_row = lax.broadcasted_iota(jnp.int32, (256, 128), 0) % 4
    flag = [jnp.where(lengths[in_req[d]] == LONGEST, 1, 0) for d in range(NI)]
    qx[...] = jnp.zeros_like(qx)
    pos[NI] = jnp.zeros((256, 128), jnp.int32)
    for d in range(NI):
        seen = [jnp.int32(0)] * 4
        for n, (place, rank) in enumerate(here):
            seen = [jnp.where((place == d) & (rank == m), positions[i * 16 + n], seen[m]) for m in range(4)]
        pos[d] = functools.reduce(lambda x, m: jnp.where(in_row == m, seen[m], x), range(1, 4), jnp.full((256, 128), seen[0]))
        pos[NI] += pos[d] * flag[d]
        qx[...] = jnp.where(jnp.full((256, 128), flag[d]) == 1, q[d].astype(jnp.float32), qx[...])

    slot_of = lax.broadcasted_iota(jnp.int32, (384, 512), 0)
    j = lax.broadcasted_iota(jnp.int32, (1, 512), 1)
    k, dt = j // 32, (t - j // 4 + 2 * 512) % NT
    found = jnp.full((384, 512), -1, jnp.int32)
    for d in range(NI):
        page = jnp.where(k < NEAR, (d * NEAR + k) * NT + dt, (NI * NEAR + k - NEAR) * NT + dt)
        goes = (j % NL == l) & (j * 64 < lengths[in_req[d]])
        to = jnp.where(goes, target_v[pl.ds(in_req[d], 1), :] - (i * NL + l) * SLOTS, -1)
        found = jnp.where(slot_of == to, page, found)
    found = jnp.max(found, axis=1, keepdims=True)
    found = jnp.where(found < 0, (NI * NEAR + FAR) * NT, found)
    eye = lax.broadcasted_iota(jnp.int32, (128, 128), 0) == lax.broadcasted_iota(jnp.int32, (128, 128), 1)
    for n in range(3):
        column_n = jnp.broadcast_to(found[n * 128 : (n + 1) * 128], (128, 128))
        index[n : n + 1, :] = jnp.sum(jnp.where(eye, column_n, 0), axis=0, keepdims=True)
    zero[...] = jnp.zeros_like(zero)

    def update(m, total, weighted, s, v):
        top = jnp.maximum(m, jnp.max(s, axis=1, keepdims=True))
        shrink = jnp.exp(m - top)
        p = jnp.exp(s - top)
        total = total * shrink + jnp.sum(p, axis=1, keepdims=True)
        weighted = weighted * shrink + jnp.dot(p.astype(jnp.bfloat16), v, preferred_element_type=jnp.float32)
        return top, total, weighted

    def dots(a, b):
        return lax.dot_general(a, b, (((1,), (1,)), ((), ())), preferred_element_type=jnp.float32) * scale

    ext_copy.wait()
    ext_out = pltpu.make_async_copy(ext, pages.at[pl.ds(NI * NEAR, FAR)], ext_sem)
    ext_out.start()

    def extra_step(k, carry):
        n = lax.broadcasted_iota(jnp.int32, (1, NT * 64), 1)
        ts = (t + NT - n // 64) % NT
        token = (((NEAR + k) * NT + ts) * NL + l) * 64 + n % 64
        s = dots(qx[...].astype(jnp.bfloat16), ext[k, :, 0].reshape(NT * 64, 128))
        s = jnp.where(token < pos[NI, :, :1], s, MASKED)
        return update(*carry, s, ext[k, :, 1].reshape(NT * 64, 128))

    empty = (
        jnp.full((256, 1), LOW, jnp.float32),
        jnp.zeros((256, 1), jnp.float32),
        jnp.zeros((256, 128), jnp.float32),
    )
    mx, tx, ax = lax.fori_loop(0, FAR, extra_step, empty)

    a = lax.broadcasted_iota(jnp.int32, (256, 16), 0)
    b = lax.broadcasted_iota(jnp.int32, (256, 16), 1)
    visible = (a % 4 == b % 4) & (b // 4 <= (a // 4) % 4) & (l == 0)
    for d in range(NI):
        rows = slice(d * 16, (d + 1) * 16)
        s = jnp.where(visible, dots(q[d], fkv[rows, :128]), MASKED)
        far = jnp.full((256, 1), flag[d]) == 1
        start = (jnp.where(far, mx, LOW), jnp.where(far, tx, 0.0), jnp.where(far, ax, 0.0))
        m, total, weighted = update(*start, s, fkv[rows, 128:])
        acc[d] = weighted
        ml[d, :, :64] = jnp.broadcast_to(m, (256, 64))
        ml[d, :, 64:] = jnp.broadcast_to(total, (256, 64))

    def visit(n, c):
        k = n % NEAR
        each(n, lambda c: c.wait_recv())

        @pl.when(n < NEAR)
        def _():
            own_copy(k).wait()

        @pl.when(n + AHEAD < 2 * NEAR)
        def _():
            issue(n + AHEAD, 0)

        def request(half, c):
            d = n // NEAR + 2 * half
            pltpu.make_async_copy(recv.at[d, k], pages.at[d * NEAR + k], page_sem.at[d, k]).start()
            column = lax.broadcasted_iota(jnp.int32, (1, NT * 64), 1)
            ts = (t + NT - column // 64) % NT
            token = ((k * NT + ts) * NL + l) * 64 + column % 64
            s = dots(q[d], recv[d, k, :, 0].reshape(NT * 64, 128))
            s = jnp.where(token < pos[d, :, :1], s, MASKED)
            m, total, weighted = update(
                ml[d, :, :1], ml[d, :, 64:65], acc[d], s, recv[d, k, :, 1].reshape(NT * 64, 128)
            )
            acc[d] = weighted
            ml[d, :, :64] = jnp.broadcast_to(m, (256, 64))
            ml[d, :, 64:] = jnp.broadcast_to(total, (256, 64))
            return c

        return lax.fori_loop(0, 2, request, c)

    eye = lax.broadcasted_iota(jnp.int32, (64, 128), 0) == lax.broadcasted_iota(jnp.int32, (64, 128), 1)

    def send_parts(stage):
        for half in range(2):
            d = stage + 2 * half
            for n in range(NL):
                rows = slice(n * 64, (n + 1) * 64)
                give[stage, n, half * 64 : (half + 1) * 64, :] = acc[d, rows, :]
                for part in range(2):
                    stat = jnp.where(eye, ml[d, rows, part * 64 : part * 64 + 1], 0.0)
                    row = 128 + half * 2 + part
                    give[stage, n, row : row + 1, :] = jnp.sum(stat, axis=0, keepdims=True)
        copies = []
        for dl in range(1, NL):
            to = column(0, dl)
            copies.append(
                pltpu.make_async_remote_copy(
                    src_ref=give.at[stage, to[1]],
                    dst_ref=got.at[stage, dl - 1],
                    send_sem=s1_sem.at[stage, dl - 1],
                    recv_sem=r1_sem.at[stage, dl - 1],
                    device_id=to,
                    device_id_type=MESH,
                )
            )
        for c in copies:
            c.start()
        return copies

    def by_x(stage, half):
        return stage == 0 or half == 0

    def spread(stage, half, phase, rows):
        along_x = by_x(stage, half) == (phase == 0)
        copies = []
        for n in range(1, NI):
            copies.append(
                pltpu.make_async_remote_copy(
                    src_ref=rows,
                    dst_ref=rows,
                    send_sem=s2_sem.at[stage, half, phase, n],
                    recv_sem=r2_sem.at[stage, half, phase, n],
                    device_id=column(n, 0) if along_x else column(0, n),
                    device_id_type=MESH,
                )
            )
        for c in copies:
            c.start()
        return copies


    def join(stage, copies):
        for c in copies:
            c.wait_recv()
        sent = []
        blocks = [give.at[stage, l]] + [got.at[stage, n] for n in range(NL - 1)]
        for half in range(2):

            def stat(block, part):
                row = 128 + half * 2 + part
                return jnp.sum(jnp.where(eye, block[row : row + 1, :], 0.0), axis=1, keepdims=True)

            tops = [stat(block, 0) for block in blocks]
            top = functools.reduce(jnp.maximum, tops)
            shares = [jnp.exp(x - top) for x in tops]
            total = sum(stat(block, 1) * share for block, share in zip(blocks, shares))
            weighted = sum(block[half * 64 : (half + 1) * 64, :] * share for block, share in zip(blocks, shares))
            joined = (weighted / total).astype(jnp.bfloat16)
            mine = l * NI + i if by_x(stage, half) else i * NL + l
            for h in range(4):
                ctx[stage, half, mine, :, h * 128 : (h + 1) * 128] = joined[h * 16 : (h + 1) * 16]
            sent.append(spread(stage, half, 0, ctx.at[stage, half, mine]))
        return sent

    def widen(stage, sent):
        wide = []
        for half in range(2):
            for c in sent[half]:
                c.wait_recv()
            at = l * NI if by_x(stage, half) else i * NL
            wide.append(spread(stage, half, 1, ctx.at[stage, half, pl.ds(at, NI)]))
        return wide

    def project(stage, wide):
        for c in wide[0] + wide[1]:
            c.wait_recv()

        def block(group, half, n):
            return ctx[stage, half, n * NI + group if by_x(stage, half) else group * NL + n]

        context = jnp.concatenate(
            [
                jnp.concatenate([block(group, half, n) for n in range(NL)], axis=1)
                for group in range(NI)
                for half in range(2)
            ],
            axis=0,
        )
        for n in range(NT // 2):
            out = jnp.dot(context, w[:, n * 256 : (n + 1) * 256], preferred_element_type=jnp.float32)
            proj[stage, 2 * n] = out[:, :128]
            proj[stage, 2 * n + 1] = out[:, 128:]
        copies = []
        for dt in range(1, NT):
            to = plane(0, dt)
            copies.append(
                pltpu.make_async_remote_copy(
                    src_ref=proj.at[stage, to[2]],
                    dst_ref=red.at[stage, dt - 1],
                    send_sem=s4_sem.at[stage, dt - 1],
                    recv_sem=r4_sem.at[stage, dt - 1],
                    device_id=to,
                    device_id_type=MESH,
                )
            )
        for c in copies:
            c.start()
        return copies

    def reduce(stage, copies):
        total = proj[stage, t]
        for n, c in enumerate(copies):
            c.wait_recv()
            total = total + red[stage, n]
        return total

    lax.fori_loop(0, 6, visit, 0)
    parts = [send_parts(0)]
    lax.fori_loop(6, 7, visit, 0)
    contexts = join(0, parts[0])
    lax.fori_loop(7, 8, visit, 0)
    wide = widen(0, contexts)
    contexts += wide
    lax.fori_loop(8, 10, visit, 0)
    w_copy.wait()
    sums = [project(0, wide)]
    lax.fori_loop(10, 12, visit, 0)
    parts.append(send_parts(1))
    first = reduce(0, sums[0])
    sent = join(1, parts[1])
    wide = widen(1, sent)
    contexts += sent + wide
    sums.append(project(1, wide))
    second = reduce(1, sums[1])

    for group in range(NI):
        value = jnp.concatenate([(first, second)[d % 2][group * 32 + d // 2 * 16 :][:16] for d in range(NI)], axis=0)
        ordered = jnp.zeros((64, 128), jnp.float32)
        for _ in range(3):
            piece = value.astype(jnp.bfloat16)
            value = value - piece.astype(jnp.float32)
            ordered += jnp.dot(back[group], piece, preferred_element_type=jnp.float32)
        own_rows = slice(group * 16, (group + 1) * 16)
        for step in range(4):
            attn[step, own_rows] = ordered[step * 16 : (step + 1) * 16] + residual[step, own_rows].astype(jnp.float32)

    zero_out = pltpu.make_async_copy(zero, pages.at[NI * NEAR + FAR], own_sem.at[0])
    zero_out.start()
    zero_out.wait()
    ext_out.wait()
    for copies in parts + contexts + sums:
        for c in copies:
            c.wait_send()

    def drain(n, c):
        each(n, lambda c: c.wait_send())
        for half in range(2):
            d = n // NEAR + 2 * half
            pltpu.make_async_copy(recv.at[d, n % NEAR], pages.at[d * NEAR + n % NEAR], page_sem.at[d, n % NEAR]).wait()
        return c

    lax.fori_loop(0, 2 * NEAR, drain, 0)


def run_main(*args):
    hbm, vmem, smem = (pl.BlockSpec(memory_space=m) for m in (pl.ANY, pltpu.VMEM, pltpu.SMEM))
    bf, f32, i32, dma = jnp.bfloat16, jnp.float32, jnp.int32, pltpu.SemaphoreType.DMA
    return pl.pallas_call(
        main_kernel,
        out_shape=(
            jax.ShapeDtypeStruct((NI * NEAR + FAR + 1, NT, 2, 64, 128), bf),
            jax.ShapeDtypeStruct((4, 64, 128), f32),
            jax.ShapeDtypeStruct((3, 128), i32),
        ),
        in_specs=[smem] * 5 + [hbm, hbm, pl.BlockSpec(memory_space=pltpu.HBM)] + [vmem] * 4,
        out_specs=(hbm, vmem, vmem),
        scratch_shapes=[
            pltpu.VMEM((SRC, 2, NT, 64, 128), bf),
            pltpu.VMEM((NI, NEAR, 2, NT, 64, 128), bf),
            pltpu.VMEM((NI, NEAR, NT, 2, 64, 128), bf),
            pltpu.VMEM((FAR, NT, 2, 64, 128), bf),
            pltpu.VMEM((2048, 1024), bf),
            pltpu.VMEM((NI, 256, 128), bf),
            pltpu.VMEM((256, 128), f32),
            pltpu.VMEM((64, 256), bf),
            pltpu.VMEM((NI + 1, 256, 128), i32),
            pltpu.VMEM((NI, 256, 128), f32),
            pltpu.VMEM((NI, 256, 128), f32),
            pltpu.VMEM((NI, 64, 64), bf),
            pltpu.SMEM((NI,), i32),
            pltpu.VMEM((2, NL, 136, 128), f32),
            pltpu.VMEM((2, NL - 1, 136, 128), f32),
            pltpu.VMEM((2, 2, NI * NL, 16, 512), bf),
            pltpu.VMEM((2, NT, 128, 128), f32),
            pltpu.VMEM((2, NT - 1, 128, 128), f32),
            pltpu.VMEM((NT, 2, 64, 128), bf),
            dma((NI, NEAR, NT)),
            dma((NI, NEAR, NT)),
            dma((NEAR,)),
            dma((NI, NEAR)),
            dma,
            dma,
            dma,
            dma((2, NL - 1)),
            dma((2, NL - 1)),
            dma((2, 2, 2, NI)),
            dma((2, 2, 2, NI)),
            dma((2, NT - 1)),
            dma((2, NT - 1)),
        ],
        compiler_params=pltpu.CompilerParams(
            collective_id=0, has_side_effects=True, vmem_limit_bytes=40 * 1024 * 1024
        ),
    )(*args)


def place_kernel(index, pages, pool, sem):
    def place(s, c):
        pltpu.make_async_copy(pages.at[index[s // 128, s % 128]], pool.at[s], sem).start()
        return c

    lax.fori_loop(0, SLOTS, place, 0, unroll=8)
    pltpu.make_async_copy(pool, pool, sem).wait()


def place_pages(index, pages):
    smem, hbm = pl.BlockSpec(memory_space=pltpu.SMEM), pl.BlockSpec(memory_space=pl.ANY)
    return pl.pallas_call(
        place_kernel,
        out_shape=jax.ShapeDtypeStruct((SLOTS, 2, 64, 128), jnp.bfloat16),
        in_specs=[smem, hbm],
        out_specs=hbm,
        scratch_shapes=[pltpu.SemaphoreType.DMA],
        compiler_params=pltpu.CompilerParams(vmem_limit_bytes=12 * 1024 * 1024),
    )(index, pages)


def shards(
    prefill_pool,
    lengths,
    src_table,
    dst_table,
    row_request,
    positions,
    queries,
    step_key_value,
    out_weight,
    residual,
):
    src, dst = src_table[:, 0], dst_table[:, 0]
    route = sum((src >= n * GROUP).astype(jnp.int32) * NI + (dst >= n * GROUP).astype(jnp.int32) for n in range(1, NI))
    extra = lax.switch(
        jnp.sum(jnp.where(lengths == LONGEST, route, 0)),
        [functools.partial(move_extra, p, g) for p in range(NI) for g in range(NI)],
        lengths,
        src_table,
        prefill_pool,
    )
    pages, attn, index = run_main(
        src_table,
        dst_table,
        lengths,
        row_request,
        positions,
        prefill_pool,
        extra,
        out_weight,
        dst_table,
        queries.reshape(64, 2048),
        step_key_value.reshape(64, 256),
        residual,
    )
    pool = place_pages(index, pages.reshape((NI * NEAR + FAR + 1) * NT, 2, 64, 128))
    return pool.reshape(SLOTS, 2, 1, 64, 128), attn


def solution(mesh):
    in_specs = (
        P(("instance", "layout", "tensor"), None, None, None, None),
        P(),
        P(),
        P(),
        P(),
        P(),
        P(None, "instance", "tensor"),
        P(None, "instance", None, "tensor", None),
        P("tensor", ("instance", "layout")),
        P(None, None, ("instance", "layout", "tensor")),
    )
    out_specs = (
        P(("instance", "layout"), None, "tensor", None, None),
        P(None, None, ("instance", "layout", "tensor")),
    )
    return jax.shard_map(shards, mesh=mesh, in_specs=in_specs, out_specs=out_specs, check_vma=False)
```

```python
import functools

import jax
import jax.numpy as jnp
from jax import lax
from jax.experimental import pallas as pl
from jax.experimental.pallas import tpu as pltpu
from jax.sharding import PartitionSpec as P

MESH = pl.DeviceIdType.MESH
LOW = -1e30
MASKED = -2e30
NI, NL, NT = 4, 4, 8
NEAR = 6
PARTS = 4
HEADS = NT // PARTS
AHEAD = 3
FAR = 10
LONGEST = 32768
SRC = 36
SLOTS = 288
GROUP = 1152


def routes(p, g):
    way = (g - p) % NI
    if way == 0:
        return [(0, FAR, [])]
    if way == 2:
        return [(0, FAR // 2, [(p + 1) % NI]), (FAR // 2, FAR, [(p - 1) % NI])]
    return [(0, FAR // 2, []), (FAR // 2, FAR, [(p - way) % NI, (p - 2 * way) % NI])]


def find(lengths):
    return functools.reduce(lambda best, r: jnp.where(lengths[r] == LONGEST, r, best), range(16), jnp.int32(0))


def extra_kernel(p, g, lengths, table, pool, dst, held, packed, hop, zero, send_sem, recv_sem, hop_send, hop_recv, fill_sem):
    i, l, t = (lax.axis_index(a) for a in ("instance", "layout", "tensor"))
    barrier = pltpu.get_barrier_semaphore()

    def hop_copy(k, part, src, to):
        return pltpu.make_async_remote_copy(
            src_ref=src,
            dst_ref=hop.at[k, part],
            send_sem=hop_send.at[k, part],
            recv_sem=hop_recv.at[k, part],
            device_id=(to, l, t),
            device_id_type=MESH,
        )

    def last_copy(k, head, src):
        dt = lax.rem(head - t + NT, NT)
        return pltpu.make_async_remote_copy(
            src_ref=src,
            dst_ref=dst.at[k, dt],
            send_sem=send_sem.at[dt, k],
            recv_sem=recv_sem.at[dt, k],
            device_id=(g, l, head),
            device_id_type=MESH,
        )

    first = 1 if p == g else 0

    for lo, hi, via in routes(p, g):
        nodes = [p] + via

        @pl.when(i == g)
        def _():
            for dt in range(first, NT):
                to = (nodes[-1], l, lax.rem(t + dt, NT))
                pl.semaphore_signal(barrier, inc=1, device_id=to, device_id_type=MESH)

        for before, after in zip(nodes, via):

            @pl.when(i == after)
            def _():
                pl.semaphore_signal(barrier, inc=1, device_id=(before, l, t), device_id_type=MESH)

    @pl.when(i == p)
    def _():
        load = pltpu.make_async_copy(pool, held, fill_sem.at[0])
        load.start()
        pl.semaphore_wait(barrier, sum(1 if via else NT - first for _, _, via in routes(p, g)))
        load.wait()
        request = find(lengths)
        rank = (i * NL + l) * NT + t

        def pack(k):
            slot = table[request, ((NEAR + k) * NT + t) * NL + l] - rank * SRC
            packed[k] = held[jnp.clip(slot, 0, SRC - 1)]

        def send(k, c):
            for lo, hi, via in reversed(routes(p, g)):

                @pl.when(lo + k < hi)
                def _():
                    pack(lo + k)
                    if via:
                        for part in range(PARTS):
                            src = packed.at[lo + k, :, part * HEADS : (part + 1) * HEADS]
                            hop_copy(lo + k, part, src, via[0]).start()
                    else:
                        for dt in range(first, NT):
                            head = lax.rem(t + dt, NT)
                            last_copy(lo + k, head, packed.at[lo + k, :, head]).start()

            return c

        lax.fori_loop(0, max(hi - lo for lo, hi, _ in routes(p, g)), send, 0)

    for lo, hi, via in routes(p, g):
        for n, node in enumerate(via):

            @pl.when(i == node)
            def _():
                pl.semaphore_wait(barrier, 1 if n + 1 < len(via) else NT)

                def forward(k, c):
                    for part in range(PARTS):
                        hop_copy(k, part, hop.at[k, part], node).wait_recv()
                        if n + 1 < len(via):
                            hop_copy(k, part, hop.at[k, part], via[n + 1]).start()
                        else:
                            for hh in range(HEADS):
                                h = lax.rem(t + hh, HEADS)
                                last_copy(k, part * HEADS + h, hop.at[k, part, :, h]).start()
                    return c

                lax.fori_loop(lo, hi, forward, 0)

    if p == g:

        @pl.when(i == g)
        def _():
            own = pltpu.make_async_copy(packed.at[:, :, t], dst.at[:, 0], fill_sem.at[0])
            own.start()
            own.wait()

    @pl.when(i != g)
    def _():
        zero[...] = jnp.zeros_like(zero)
        fills = [pltpu.make_async_copy(zero, dst.at[k], fill_sem.at[k]) for k in range(FAR)]
        for f in fills:
            f.start()
        for f in fills:
            f.wait()

    for lo, hi, via in routes(p, g):
        nodes = [p] + via
        for n, node in enumerate(nodes):

            @pl.when(i == node)
            def _():
                def drain(k, c):
                    if n + 1 < len(nodes):
                        for part in range(PARTS):
                            hop_copy(k, part, hop.at[k, part], node).wait_send()
                    else:
                        for dt in range(first, NT):
                            head = lax.rem(t + dt, NT)
                            last_copy(k, head, packed.at[k, :, head]).wait_send()
                    return c

                lax.fori_loop(lo, hi, drain, 0)

    @pl.when(i == g)
    def _():
        def arrive(k, c):
            for dt in range(first, NT):
                head = lax.rem(t + dt, NT)
                last_copy(k, head, packed.at[k, :, head]).wait_recv()
            return c

        lax.fori_loop(0, FAR, arrive, 0)


def move_extra(p, g, lengths, table, pool):
    smem, hbm = pl.BlockSpec(memory_space=pltpu.SMEM), pl.BlockSpec(memory_space=pl.ANY)
    bf, dma = jnp.bfloat16, pltpu.SemaphoreType.DMA
    return pl.pallas_call(
        functools.partial(extra_kernel, p, g),
        out_shape=jax.ShapeDtypeStruct((FAR, NT, 2, 64, 128), bf),
        in_specs=[smem, smem, hbm],
        out_specs=hbm,
        scratch_shapes=[
            pltpu.VMEM((SRC, 2, NT, 64, 128), bf),
            pltpu.VMEM((FAR, 2, NT, 64, 128), bf),
            pltpu.VMEM((FAR, PARTS, 2, HEADS, 64, 128), bf),
            pltpu.VMEM((NT, 2, 64, 128), bf),
            dma((NT, FAR)),
            dma((NT, FAR)),
            dma((FAR, PARTS)),
            dma((FAR, PARTS)),
            dma((FAR,)),
        ],
        compiler_params=pltpu.CompilerParams(
            collective_id=1 + p * NI + g, has_side_effects=True, vmem_limit_bytes=32 * 1024 * 1024
        ),
    )(lengths, table, pool)


def main_kernel(
    table,
    target,
    lengths,
    row_request,
    positions,
    pool,
    extra,
    weight,
    target_v,
    query,
    fresh,
    residual,
    pages,
    attn,
    index,
    held,
    send,
    recv,
    ext,
    w,
    q,
    qx,
    fkv,
    pos,
    acc,
    ml,
    back,
    reqs,
    give,
    got,
    ctx,
    proj,
    red,
    zero,
    send_sem,
    recv_sem,
    own_sem,
    page_sem,
    w_sem,
    ext_sem,
    pool_sem,
    s1_sem,
    r1_sem,
    s2_sem,
    r2_sem,
    s4_sem,
    r4_sem,
):
    i, l, t = (lax.axis_index(a) for a in ("instance", "layout", "tensor"))
    scale = 128.0**-0.5

    def plane(di, dt):
        return (lax.rem(i + di, NI), l, lax.rem(t + dt, NT))

    def column(di, dl):
        return (lax.rem(i + di, NI), lax.rem(l + dl, NL), t)

    barrier = pltpu.get_barrier_semaphore()
    load = pltpu.make_async_copy(pool, held, pool_sem)
    load.start()
    for di in range(NI):
        for dt in range(NT):
            if di or dt:
                pl.semaphore_signal(barrier, inc=1, device_id=plane(di, dt), device_id_type=MESH)
    for di in range(NI):
        for dl in range(1, NL):
            pl.semaphore_signal(barrier, inc=1, device_id=column(di, dl), device_id_type=MESH)

    w_copy = pltpu.make_async_copy(weight, w, w_sem)
    ext_copy = pltpu.make_async_copy(extra, ext, ext_sem)
    ext_copy.start()

    def own_copy(k):
        return pltpu.make_async_copy(send.at[0, k, :, t], recv.at[0, k, 0], own_sem.at[k])

    out_req = [jnp.int32(0)] * NI
    in_req = [jnp.int32(0)] * NI
    for r in range(16):
        src_r, dst_r = lax.div(table[r, 0], GROUP), lax.div(target[r, 0], GROUP)
        for d in range(NI):
            out_req[d] = jnp.where((src_r == i) & (dst_r == lax.rem(i + d, NI)), r, out_req[d])
            in_req[d] = jnp.where((dst_r == i) & (src_r == lax.rem(i + NI - d, NI)), r, in_req[d])
    for d in range(NI):
        reqs[d] = out_req[d]
    base = ((i * NL + l) * NT + t) * SRC
    pl.semaphore_wait(barrier, NI * NT - 1 + NI * (NL - 1))
    load.wait()

    def page_copy(k, di, dt):
        to = plane(di, dt)
        return pltpu.make_async_remote_copy(
            src_ref=send.at[di, k, :, to[2]],
            dst_ref=recv.at[di, k, dt],
            send_sem=send_sem.at[di, k, dt],
            recv_sem=recv_sem.at[di, k, dt],
            device_id=to,
            device_id_type=MESH,
        )

    def pair(n, m):
        d = n // NEAR + 2 * ((m // 2) % 2)
        return d, ((d + m // 4) % 4) * 2 + m % 2

    def each(n, act):
        def one(m, c):
            d, dt = pair(n, m)

            @pl.when((d != 0) | (dt != 0))
            def _():
                act(page_copy(n % NEAR, d, dt))

            return c

        lax.fori_loop(0, 16, one, 0)

    def issue(n, c):
        k = n % NEAR
        for half in range(2):
            d = n // NEAR + 2 * half
            slot = table[reqs[d], (k * NT + t) * NL + l] - base
            send[d, k] = held[jnp.clip(slot, 0, SRC - 1)]
        each(n, lambda c: c.start())

        @pl.when(n < NEAR)
        def _():
            own_copy(k).start()

        return c

    lax.fori_loop(0, AHEAD, issue, 0)
    w_copy.start()

    def places(group):
        count, found = [jnp.int32(0)] * NI, []
        for n in range(16):
            request = row_request[group * 16 + n]
            d = lax.rem(group - lax.div(table[request, 0], GROUP) + NI, NI)
            rank = functools.reduce(lambda x, m: jnp.where(d == m, count[m], x), range(1, NI), count[0])
            count = [jnp.where(d == m, count[m] + 1, count[m]) for m in range(NI)]
            found.append((d, rank))
        return found

    def one_hot(found, by, plain):
        step = plain // 16
        hit = functools.reduce(
            jnp.logical_or, [(plain % 16 == n) & (by - step * 4 == d * 16 + rank) for n, (d, rank) in enumerate(found)]
        )
        return jnp.where(hit, 1.0, 0.0).astype(jnp.bfloat16)

    down = lax.broadcasted_iota(jnp.int32, (64, 64), 0)
    across = lax.broadcasted_iota(jnp.int32, (64, 64), 1)
    here = places(i)
    pick = one_hot(here, down, across)

    for group in range(NI):
        back[group] = one_hot(places(jnp.int32(group)), across, down)

    sorted_q = jnp.dot(pick, query[...], preferred_element_type=jnp.float32).astype(jnp.bfloat16)
    fkv[...] = jnp.dot(pick, fresh[...], preferred_element_type=jnp.float32).astype(jnp.bfloat16)
    for h in range(16):
        for d in range(NI):
            q[d, h * 16 : (h + 1) * 16, :] = sorted_q[d * 16 : (d + 1) * 16, h * 128 : (h + 1) * 128]
    in_row = lax.broadcasted_iota(jnp.int32, (256, 128), 0) % 4
    flag = [jnp.where(lengths[in_req[d]] == LONGEST, 1, 0) for d in range(NI)]
    qx[...] = jnp.zeros_like(qx)
    pos[NI] = jnp.zeros((256, 128), jnp.int32)
    for d in range(NI):
        seen = [jnp.int32(0)] * 4
        for n, (place, rank) in enumerate(here):
            seen = [jnp.where((place == d) & (rank == m), positions[i * 16 + n], seen[m]) for m in range(4)]
        pos[d] = functools.reduce(lambda x, m: jnp.where(in_row == m, seen[m], x), range(1, 4), jnp.full((256, 128), seen[0]))
        pos[NI] += pos[d] * flag[d]
        qx[...] = jnp.where(jnp.full((256, 128), flag[d]) == 1, q[d].astype(jnp.float32), qx[...])

    slot_of = lax.broadcasted_iota(jnp.int32, (384, 512), 0)
    j = lax.broadcasted_iota(jnp.int32, (1, 512), 1)
    k, dt = j // 32, (t - j // 4 + 2 * 512) % NT
    found = jnp.full((384, 512), -1, jnp.int32)
    for d in range(NI):
        page = jnp.where(k < NEAR, (d * NEAR + k) * NT + dt, (NI * NEAR + k - NEAR) * NT + dt)
        goes = (j % NL == l) & (j * 64 < lengths[in_req[d]])
        to = jnp.where(goes, target_v[pl.ds(in_req[d], 1), :] - (i * NL + l) * SLOTS, -1)
        found = jnp.where(slot_of == to, page, found)
    found = jnp.max(found, axis=1, keepdims=True)
    found = jnp.where(found < 0, (NI * NEAR + FAR) * NT, found)
    eye = lax.broadcasted_iota(jnp.int32, (128, 128), 0) == lax.broadcasted_iota(jnp.int32, (128, 128), 1)
    for n in range(3):
        column_n = jnp.broadcast_to(found[n * 128 : (n + 1) * 128], (128, 128))
        index[n : n + 1, :] = jnp.sum(jnp.where(eye, column_n, 0), axis=0, keepdims=True)
    zero[...] = jnp.zeros_like(zero)
    zero_out = pltpu.make_async_copy(zero, pages.at[NI * NEAR + FAR], own_sem.at[NEAR])
    zero_out.start()

    def update(m, total, weighted, s, v):
        top = jnp.maximum(m, jnp.max(s, axis=1, keepdims=True))
        shrink = jnp.exp(m - top)
        p = jnp.exp(s - top)
        total = total * shrink + jnp.sum(p, axis=1, keepdims=True)
        weighted = weighted * shrink + jnp.dot(p.astype(jnp.bfloat16), v, preferred_element_type=jnp.float32)
        return top, total, weighted

    def dots(a, b):
        return lax.dot_general(a, b, (((1,), (1,)), ((), ())), preferred_element_type=jnp.float32) * scale

    ext_copy.wait()
    ext_out = pltpu.make_async_copy(ext, pages.at[pl.ds(NI * NEAR, FAR)], ext_sem)
    ext_out.start()

    def extra_step(k, carry):
        n = lax.broadcasted_iota(jnp.int32, (1, NT * 64), 1)
        ts = (t + NT - n // 64) % NT
        token = (((NEAR + k) * NT + ts) * NL + l) * 64 + n % 64
        s = dots(qx[...].astype(jnp.bfloat16), ext[k, :, 0].reshape(NT * 64, 128))
        s = jnp.where(token < pos[NI, :, :1], s, MASKED)
        return update(*carry, s, ext[k, :, 1].reshape(NT * 64, 128))

    empty = (
        jnp.full((256, 1), LOW, jnp.float32),
        jnp.zeros((256, 1), jnp.float32),
        jnp.zeros((256, 128), jnp.float32),
    )
    mx, tx, ax = lax.fori_loop(0, FAR, extra_step, empty)

    a = lax.broadcasted_iota(jnp.int32, (256, 16), 0)
    b = lax.broadcasted_iota(jnp.int32, (256, 16), 1)
    visible = (a % 4 == b % 4) & (b // 4 <= (a // 4) % 4) & (l == 0)
    for d in range(NI):
        rows = slice(d * 16, (d + 1) * 16)
        s = jnp.where(visible, dots(q[d], fkv[rows, :128]), MASKED)
        far = jnp.full((256, 1), flag[d]) == 1
        start = (jnp.where(far, mx, LOW), jnp.where(far, tx, 0.0), jnp.where(far, ax, 0.0))
        m, total, weighted = update(*start, s, fkv[rows, 128:])
        acc[d] = weighted
        ml[d, :, :64] = jnp.broadcast_to(m, (256, 64))
        ml[d, :, 64:] = jnp.broadcast_to(total, (256, 64))

    def drain(n, c):
        each(n, lambda c: c.wait_send())
        for half in range(2):
            d = n // NEAR + 2 * half
            pltpu.make_async_copy(recv.at[d, n % NEAR], pages.at[d * NEAR + n % NEAR], page_sem.at[d, n % NEAR]).wait()
        return c

    def visit(n, c):
        k = n % NEAR
        each(n, lambda c: c.wait_recv())

        @pl.when(n < NEAR)
        def _():
            own_copy(k).wait()

        @pl.when(n + AHEAD < 2 * NEAR)
        def _():
            issue(n + AHEAD, 0)

        def request(half, c):
            d = n // NEAR + 2 * half
            pltpu.make_async_copy(recv.at[d, k], pages.at[d * NEAR + k], page_sem.at[d, k]).start()
            column = lax.broadcasted_iota(jnp.int32, (1, NT * 64), 1)
            ts = (t + NT - column // 64) % NT
            token = ((k * NT + ts) * NL + l) * 64 + column % 64
            s = dots(q[d], recv[d, k, :, 0].reshape(NT * 64, 128))
            s = jnp.where(token < pos[d, :, :1], s, MASKED)
            m, total, weighted = update(
                ml[d, :, :1], ml[d, :, 64:65], acc[d], s, recv[d, k, :, 1].reshape(NT * 64, 128)
            )
            acc[d] = weighted
            ml[d, :, :64] = jnp.broadcast_to(m, (256, 64))
            ml[d, :, 64:] = jnp.broadcast_to(total, (256, 64))
            return c

        lax.fori_loop(0, 2, request, 0)

        @pl.when(n >= NEAR)
        def _():
            drain(n - NEAR, 0)

        return c

    eye = lax.broadcasted_iota(jnp.int32, (64, 128), 0) == lax.broadcasted_iota(jnp.int32, (64, 128), 1)

    def send_parts(stage):
        for half in range(2):
            d = stage + 2 * half
            for n in range(NL):
                rows = slice(n * 64, (n + 1) * 64)
                give[stage, n, half * 64 : (half + 1) * 64, :] = acc[d, rows, :]
                for part in range(2):
                    stat = jnp.where(eye, ml[d, rows, part * 64 : part * 64 + 1], 0.0)
                    row = 128 + half * 2 + part
                    give[stage, n, row : row + 1, :] = jnp.sum(stat, axis=0, keepdims=True)
        copies = []
        for dl in range(1, NL):
            to = column(0, dl)
            copies.append(
                pltpu.make_async_remote_copy(
                    src_ref=give.at[stage, to[1]],
                    dst_ref=got.at[stage, dl - 1],
                    send_sem=s1_sem.at[stage, dl - 1],
                    recv_sem=r1_sem.at[stage, dl - 1],
                    device_id=to,
                    device_id_type=MESH,
                )
            )
        for c in copies:
            c.start()
        return copies

    def by_x(stage, half):
        return stage == 0 or half == 0

    def spread(stage, half, phase, rows):
        along_x = by_x(stage, half) == (phase == 0)
        copies = []
        for n in range(1, NI):
            copies.append(
                pltpu.make_async_remote_copy(
                    src_ref=rows,
                    dst_ref=rows,
                    send_sem=s2_sem.at[stage, half, phase, n],
                    recv_sem=r2_sem.at[stage, half, phase, n],
                    device_id=column(n, 0) if along_x else column(0, n),
                    device_id_type=MESH,
                )
            )
        for c in copies:
            c.start()
        return copies


    def join(stage, copies):
        for c in copies:
            c.wait_recv()
        sent = []
        blocks = [give.at[stage, l]] + [got.at[stage, n] for n in range(NL - 1)]
        for half in range(2):

            def stat(block, part):
                row = 128 + half * 2 + part
                return jnp.sum(jnp.where(eye, block[row : row + 1, :], 0.0), axis=1, keepdims=True)

            tops = [stat(block, 0) for block in blocks]
            top = functools.reduce(jnp.maximum, tops)
            shares = [jnp.exp(x - top) for x in tops]
            total = sum(stat(block, 1) * share for block, share in zip(blocks, shares))
            weighted = sum(block[half * 64 : (half + 1) * 64, :] * share for block, share in zip(blocks, shares))
            joined = (weighted / total).astype(jnp.bfloat16)
            mine = l * NI + i if by_x(stage, half) else i * NL + l
            for h in range(4):
                ctx[stage, half, mine, :, h * 128 : (h + 1) * 128] = joined[h * 16 : (h + 1) * 16]
            sent.append(spread(stage, half, 0, ctx.at[stage, half, mine]))
        return sent

    def widen(stage, sent):
        wide = []
        for half in range(2):
            for c in sent[half]:
                c.wait_recv()
            at = l * NI if by_x(stage, half) else i * NL
            wide.append(spread(stage, half, 1, ctx.at[stage, half, pl.ds(at, NI)]))
        return wide

    def project(stage, wide):
        for c in wide[0] + wide[1]:
            c.wait_recv()

        def block(group, half, n):
            return ctx[stage, half, n * NI + group if by_x(stage, half) else group * NL + n]

        context = jnp.concatenate(
            [
                jnp.concatenate([block(group, half, n) for n in range(NL)], axis=1)
                for group in range(NI)
                for half in range(2)
            ],
            axis=0,
        )
        for n in range(NT // 2):
            out = jnp.dot(context, w[:, n * 256 : (n + 1) * 256], preferred_element_type=jnp.float32)
            proj[stage, 2 * n] = out[:, :128]
            proj[stage, 2 * n + 1] = out[:, 128:]
        copies = []
        for dt in range(1, NT):
            to = plane(0, dt)
            copies.append(
                pltpu.make_async_remote_copy(
                    src_ref=proj.at[stage, to[2]],
                    dst_ref=red.at[stage, dt - 1],
                    send_sem=s4_sem.at[stage, dt - 1],
                    recv_sem=r4_sem.at[stage, dt - 1],
                    device_id=to,
                    device_id_type=MESH,
                )
            )
        for c in copies:
            c.start()
        return copies

    def reduce(stage, copies):
        total = proj[stage, t]
        for n, c in enumerate(copies):
            c.wait_recv()
            total = total + red[stage, n]
        return total

    lax.fori_loop(0, 6, visit, 0)
    parts = [send_parts(0)]
    lax.fori_loop(6, 7, visit, 0)
    contexts = join(0, parts[0])
    lax.fori_loop(7, 8, visit, 0)
    wide = widen(0, contexts)
    contexts += wide
    lax.fori_loop(8, 10, visit, 0)
    w_copy.wait()
    sums = [project(0, wide)]
    lax.fori_loop(10, 12, visit, 0)
    parts.append(send_parts(1))
    first = reduce(0, sums[0])
    lax.fori_loop(6, 9, drain, 0)
    sent = join(1, parts[1])
    for copies in [zero_out, ext_out]:
        copies.wait()
    for copies in parts + contexts:
        for c in copies:
            c.wait_send()
    wide = widen(1, sent)
    lax.fori_loop(9, 12, drain, 0)
    sums.append(project(1, wide))
    for copies in sent + wide:
        for c in copies:
            c.wait_send()
    second = reduce(1, sums[1])

    for group in range(NI):
        value = jnp.concatenate([(first, second)[d % 2][group * 32 + d // 2 * 16 :][:16] for d in range(NI)], axis=0)
        ordered = jnp.zeros((64, 128), jnp.float32)
        for _ in range(3):
            piece = value.astype(jnp.bfloat16)
            value = value - piece.astype(jnp.float32)
            ordered += jnp.dot(back[group], piece, preferred_element_type=jnp.float32)
        own_rows = slice(group * 16, (group + 1) * 16)
        for step in range(4):
            attn[step, own_rows] = ordered[step * 16 : (step + 1) * 16] + residual[step, own_rows].astype(jnp.float32)

    for copies in sums:
        for c in copies:
            c.wait_send()


def run_main(*args):
    hbm, vmem, smem = (pl.BlockSpec(memory_space=m) for m in (pl.ANY, pltpu.VMEM, pltpu.SMEM))
    bf, f32, i32, dma = jnp.bfloat16, jnp.float32, jnp.int32, pltpu.SemaphoreType.DMA
    return pl.pallas_call(
        main_kernel,
        out_shape=(
            jax.ShapeDtypeStruct((NI * NEAR + FAR + 1, NT, 2, 64, 128), bf),
            jax.ShapeDtypeStruct((4, 64, 128), f32),
            jax.ShapeDtypeStruct((3, 128), i32),
        ),
        in_specs=[smem] * 5 + [hbm, hbm, pl.BlockSpec(memory_space=pltpu.HBM)] + [vmem] * 4,
        out_specs=(hbm, vmem, vmem),
        scratch_shapes=[
            pltpu.VMEM((SRC, 2, NT, 64, 128), bf),
            pltpu.VMEM((NI, NEAR, 2, NT, 64, 128), bf),
            pltpu.VMEM((NI, NEAR, NT, 2, 64, 128), bf),
            pltpu.VMEM((FAR, NT, 2, 64, 128), bf),
            pltpu.VMEM((2048, 1024), bf),
            pltpu.VMEM((NI, 256, 128), bf),
            pltpu.VMEM((256, 128), f32),
            pltpu.VMEM((64, 256), bf),
            pltpu.VMEM((NI + 1, 256, 128), i32),
            pltpu.VMEM((NI, 256, 128), f32),
            pltpu.VMEM((NI, 256, 128), f32),
            pltpu.VMEM((NI, 64, 64), bf),
            pltpu.SMEM((NI,), i32),
            pltpu.VMEM((2, NL, 136, 128), f32),
            pltpu.VMEM((2, NL - 1, 136, 128), f32),
            pltpu.VMEM((2, 2, NI * NL, 16, 512), bf),
            pltpu.VMEM((2, NT, 128, 128), f32),
            pltpu.VMEM((2, NT - 1, 128, 128), f32),
            pltpu.VMEM((NT, 2, 64, 128), bf),
            dma((NI, NEAR, NT)),
            dma((NI, NEAR, NT)),
            dma((NEAR + 1,)),
            dma((NI, NEAR)),
            dma,
            dma,
            dma,
            dma((2, NL - 1)),
            dma((2, NL - 1)),
            dma((2, 2, 2, NI)),
            dma((2, 2, 2, NI)),
            dma((2, NT - 1)),
            dma((2, NT - 1)),
        ],
        compiler_params=pltpu.CompilerParams(
            collective_id=0, has_side_effects=True, vmem_limit_bytes=40 * 1024 * 1024
        ),
    )(*args)


def place_kernel(index, pages, pool, sem):
    def place(s, c):
        pltpu.make_async_copy(pages.at[index[s // 128, s % 128]], pool.at[s], sem).start()
        return c

    lax.fori_loop(0, SLOTS, place, 0, unroll=8)
    pltpu.make_async_copy(pool, pool, sem).wait()


def place_pages(index, pages):
    smem, hbm = pl.BlockSpec(memory_space=pltpu.SMEM), pl.BlockSpec(memory_space=pl.ANY)
    return pl.pallas_call(
        place_kernel,
        out_shape=jax.ShapeDtypeStruct((SLOTS, 2, 64, 128), jnp.bfloat16),
        in_specs=[smem, hbm],
        out_specs=hbm,
        scratch_shapes=[pltpu.SemaphoreType.DMA],
        compiler_params=pltpu.CompilerParams(vmem_limit_bytes=12 * 1024 * 1024),
    )(index, pages)


def shards(
    prefill_pool,
    lengths,
    src_table,
    dst_table,
    row_request,
    positions,
    queries,
    step_key_value,
    out_weight,
    residual,
):
    src, dst = src_table[:, 0], dst_table[:, 0]
    route = sum((src >= n * GROUP).astype(jnp.int32) * NI + (dst >= n * GROUP).astype(jnp.int32) for n in range(1, NI))
    extra = lax.switch(
        jnp.sum(jnp.where(lengths == LONGEST, route, 0)),
        [functools.partial(move_extra, p, g) for p in range(NI) for g in range(NI)],
        lengths,
        src_table,
        prefill_pool,
    )
    pages, attn, index = run_main(
        src_table,
        dst_table,
        lengths,
        row_request,
        positions,
        prefill_pool,
        extra,
        out_weight,
        dst_table,
        queries.reshape(64, 2048),
        step_key_value.reshape(64, 256),
        residual,
    )
    pool = place_pages(index, pages.reshape((NI * NEAR + FAR + 1) * NT, 2, 64, 128))
    return pool.reshape(SLOTS, 2, 1, 64, 128), attn


def solution(mesh):
    in_specs = (
        P(("instance", "layout", "tensor"), None, None, None, None),
        P(),
        P(),
        P(),
        P(),
        P(),
        P(None, "instance", "tensor"),
        P(None, "instance", None, "tensor", None),
        P("tensor", ("instance", "layout")),
        P(None, None, ("instance", "layout", "tensor")),
    )
    out_specs = (
        P(("instance", "layout"), None, "tensor", None, None),
        P(None, None, ("instance", "layout", "tensor")),
    )
    return jax.shard_map(shards, mesh=mesh, in_specs=in_specs, out_specs=out_specs, check_vma=False)
```

```python
import functools

import jax
import jax.numpy as jnp
from jax import lax
from jax.experimental import pallas as pl
from jax.experimental.pallas import tpu as pltpu
from jax.sharding import PartitionSpec as P

MESH = pl.DeviceIdType.MESH
LOW = -1e30
MASKED = -2e30
NI, NL, NT = 4, 4, 8
NEAR = 6
PARTS = 4
HEADS = NT // PARTS
AHEAD = 3
FAR = 10
LONGEST = 32768
SRC = 36
SLOTS = 288
GROUP = 1152


def routes(p, g):
    way = (g - p) % NI
    if way == 0:
        return [(0, FAR, [])]
    if way == 2:
        return [(0, FAR // 2, [(p + 1) % NI]), (FAR // 2, FAR, [(p - 1) % NI])]
    return [(0, FAR // 2, []), (FAR // 2, FAR, [(p - way) % NI, (p - 2 * way) % NI])]


def find(lengths):
    return functools.reduce(lambda best, r: jnp.where(lengths[r] == LONGEST, r, best), range(16), jnp.int32(0))


def extra_kernel(p, g, lengths, table, pool, dst, held, packed, hop, zero, send_sem, recv_sem, hop_send, hop_recv, fill_sem):
    i, l, t = (lax.axis_index(a) for a in ("instance", "layout", "tensor"))
    barrier = pltpu.get_barrier_semaphore()

    def hop_copy(k, part, src, to):
        return pltpu.make_async_remote_copy(
            src_ref=src,
            dst_ref=hop.at[k, part],
            send_sem=hop_send.at[k, part],
            recv_sem=hop_recv.at[k, part],
            device_id=(to, l, t),
            device_id_type=MESH,
        )

    def last_copy(k, head, src):
        dt = lax.rem(head - t + NT, NT)
        return pltpu.make_async_remote_copy(
            src_ref=src,
            dst_ref=dst.at[k, dt],
            send_sem=send_sem.at[dt, k],
            recv_sem=recv_sem.at[dt, k],
            device_id=(g, l, head),
            device_id_type=MESH,
        )

    first = 1 if p == g else 0

    for lo, hi, via in routes(p, g):
        nodes = [p] + via

        @pl.when(i == g)
        def _():
            for dt in range(first, NT):
                to = (nodes[-1], l, lax.rem(t + dt, NT))
                pl.semaphore_signal(barrier, inc=1, device_id=to, device_id_type=MESH)

        for before, after in zip(nodes, via):

            @pl.when(i == after)
            def _():
                pl.semaphore_signal(barrier, inc=1, device_id=(before, l, t), device_id_type=MESH)

    @pl.when(i == p)
    def _():
        load = pltpu.make_async_copy(pool, held, fill_sem.at[0])
        load.start()
        pl.semaphore_wait(barrier, sum(1 if via else NT - first for _, _, via in routes(p, g)))
        load.wait()
        request = find(lengths)
        rank = (i * NL + l) * NT + t

        def pack(k):
            slot = table[request, ((NEAR + k) * NT + t) * NL + l] - rank * SRC
            packed[k] = held[jnp.clip(slot, 0, SRC - 1)]

        def send(k, c):
            for lo, hi, via in reversed(routes(p, g)):

                @pl.when(lo + k < hi)
                def _():
                    pack(lo + k)
                    if via:
                        for part in range(PARTS):
                            src = packed.at[lo + k, :, part * HEADS : (part + 1) * HEADS]
                            hop_copy(lo + k, part, src, via[0]).start()
                    else:
                        for dt in range(first, NT):
                            head = lax.rem(t + dt, NT)
                            last_copy(lo + k, head, packed.at[lo + k, :, head]).start()

            return c

        lax.fori_loop(0, max(hi - lo for lo, hi, _ in routes(p, g)), send, 0)

    for lo, hi, via in routes(p, g):
        for n, node in enumerate(via):

            @pl.when(i == node)
            def _():
                pl.semaphore_wait(barrier, 1 if n + 1 < len(via) else NT)

                def forward(k, c):
                    for part in range(PARTS):
                        hop_copy(k, part, hop.at[k, part], node).wait_recv()
                        if n + 1 < len(via):
                            hop_copy(k, part, hop.at[k, part], via[n + 1]).start()
                        else:
                            for hh in range(HEADS):
                                h = lax.rem(t + hh, HEADS)
                                last_copy(k, part * HEADS + h, hop.at[k, part, :, h]).start()
                    return c

                lax.fori_loop(lo, hi, forward, 0)

    if p == g:

        @pl.when(i == g)
        def _():
            own = pltpu.make_async_copy(packed.at[:, :, t], dst.at[:, 0], fill_sem.at[0])
            own.start()
            own.wait()

    @pl.when(i != g)
    def _():
        zero[...] = jnp.zeros_like(zero)
        fills = [pltpu.make_async_copy(zero, dst.at[k], fill_sem.at[k]) for k in range(FAR)]
        for f in fills:
            f.start()
        for f in fills:
            f.wait()

    for lo, hi, via in routes(p, g):
        nodes = [p] + via
        for n, node in enumerate(nodes):

            @pl.when(i == node)
            def _():
                def drain(k, c):
                    if n + 1 < len(nodes):
                        for part in range(PARTS):
                            hop_copy(k, part, hop.at[k, part], node).wait_send()
                    else:
                        for dt in range(first, NT):
                            head = lax.rem(t + dt, NT)
                            last_copy(k, head, packed.at[k, :, head]).wait_send()
                    return c

                lax.fori_loop(lo, hi, drain, 0)

    @pl.when(i == g)
    def _():
        def arrive(k, c):
            for dt in range(first, NT):
                head = lax.rem(t + dt, NT)
                last_copy(k, head, packed.at[k, :, head]).wait_recv()
            return c

        lax.fori_loop(0, FAR, arrive, 0)


def move_extra(p, g, lengths, table, pool):
    smem, hbm = pl.BlockSpec(memory_space=pltpu.SMEM), pl.BlockSpec(memory_space=pl.ANY)
    bf, dma = jnp.bfloat16, pltpu.SemaphoreType.DMA
    return pl.pallas_call(
        functools.partial(extra_kernel, p, g),
        out_shape=jax.ShapeDtypeStruct((FAR, NT, 2, 64, 128), bf),
        in_specs=[smem, smem, hbm],
        out_specs=hbm,
        scratch_shapes=[
            pltpu.VMEM((SRC, 2, NT, 64, 128), bf),
            pltpu.VMEM((FAR, 2, NT, 64, 128), bf),
            pltpu.VMEM((FAR, PARTS, 2, HEADS, 64, 128), bf),
            pltpu.VMEM((NT, 2, 64, 128), bf),
            dma((NT, FAR)),
            dma((NT, FAR)),
            dma((FAR, PARTS)),
            dma((FAR, PARTS)),
            dma((FAR,)),
        ],
        compiler_params=pltpu.CompilerParams(
            collective_id=1 + p * NI + g, has_side_effects=True, vmem_limit_bytes=32 * 1024 * 1024
        ),
    )(lengths, table, pool)


def main_kernel(
    table,
    target,
    lengths,
    row_request,
    positions,
    pool,
    extra,
    weight,
    target_v,
    query,
    fresh,
    residual,
    pages,
    attn,
    index,
    held,
    send,
    recv,
    ext,
    w,
    q,
    qx,
    fkv,
    pos,
    acc,
    ml,
    back,
    reqs,
    give,
    got,
    ctx,
    proj,
    red,
    zero,
    send_sem,
    recv_sem,
    own_sem,
    page_sem,
    w_sem,
    ext_sem,
    pool_sem,
    s1_sem,
    r1_sem,
    s2_sem,
    r2_sem,
    s4_sem,
    r4_sem,
):
    i, l, t = (lax.axis_index(a) for a in ("instance", "layout", "tensor"))
    scale = 128.0**-0.5

    def plane(di, dt):
        return (lax.rem(i + di, NI), l, lax.rem(t + dt, NT))

    def column(di, dl):
        return (lax.rem(i + di, NI), lax.rem(l + dl, NL), t)

    barrier = pltpu.get_barrier_semaphore()
    load = pltpu.make_async_copy(pool, held, pool_sem)
    load.start()
    for di in range(NI):
        for dt in range(NT):
            if di or dt:
                pl.semaphore_signal(barrier, inc=1, device_id=plane(di, dt), device_id_type=MESH)
    for di in range(NI):
        for dl in range(1, NL):
            pl.semaphore_signal(barrier, inc=1, device_id=column(di, dl), device_id_type=MESH)

    w_copy = pltpu.make_async_copy(weight, w, w_sem)
    ext_copy = pltpu.make_async_copy(extra, ext, ext_sem)
    ext_copy.start()

    def own_copy(k):
        return pltpu.make_async_copy(send.at[0, k, :, t], recv.at[0, k, 0], own_sem.at[k])

    out_req = [jnp.int32(0)] * NI
    in_req = [jnp.int32(0)] * NI
    for r in range(16):
        src_r, dst_r = lax.div(table[r, 0], GROUP), lax.div(target[r, 0], GROUP)
        for d in range(NI):
            out_req[d] = jnp.where((src_r == i) & (dst_r == lax.rem(i + d, NI)), r, out_req[d])
            in_req[d] = jnp.where((dst_r == i) & (src_r == lax.rem(i + NI - d, NI)), r, in_req[d])
    for d in range(NI):
        reqs[d] = out_req[d]
    base = ((i * NL + l) * NT + t) * SRC
    pl.semaphore_wait(barrier, NI * NT - 1 + NI * (NL - 1))
    load.wait()

    def page_copy(k, di, dt):
        to = plane(di, dt)
        return pltpu.make_async_remote_copy(
            src_ref=send.at[di, k, :, to[2]],
            dst_ref=recv.at[di, k, dt],
            send_sem=send_sem.at[di, k, dt],
            recv_sem=recv_sem.at[di, k, dt],
            device_id=to,
            device_id_type=MESH,
        )

    def pair(n, m):
        d = n // NEAR + 2 * ((m // 2) % 2)
        return d, ((d + m // 4) % 4) * 2 + m % 2

    def each(n, act):
        def one(m, c):
            d, dt = pair(n, m)

            @pl.when((d != 0) | (dt != 0))
            def _():
                act(page_copy(n % NEAR, d, dt))

            return c

        lax.fori_loop(0, 16, one, 0)

    def issue(n, c):
        k = n % NEAR
        for half in range(2):
            d = n // NEAR + 2 * half
            slot = table[reqs[d], (k * NT + t) * NL + l] - base
            send[d, k] = held[jnp.clip(slot, 0, SRC - 1)]
        each(n, lambda c: c.start())

        @pl.when(n < NEAR)
        def _():
            own_copy(k).start()

        return c

    lax.fori_loop(0, AHEAD, issue, 0)
    w_copy.start()

    def places(group):
        count, found = [jnp.int32(0)] * NI, []
        for n in range(16):
            request = row_request[group * 16 + n]
            d = lax.rem(group - lax.div(table[request, 0], GROUP) + NI, NI)
            rank = functools.reduce(lambda x, m: jnp.where(d == m, count[m], x), range(1, NI), count[0])
            count = [jnp.where(d == m, count[m] + 1, count[m]) for m in range(NI)]
            found.append((d, rank))
        return found

    def one_hot(found, by, plain):
        step = plain // 16
        hit = functools.reduce(
            jnp.logical_or, [(plain % 16 == n) & (by - step * 4 == d * 16 + rank) for n, (d, rank) in enumerate(found)]
        )
        return jnp.where(hit, 1.0, 0.0).astype(jnp.bfloat16)

    down = lax.broadcasted_iota(jnp.int32, (64, 64), 0)
    across = lax.broadcasted_iota(jnp.int32, (64, 64), 1)
    here = places(i)
    pick = one_hot(here, down, across)

    for group in range(NI):
        back[group] = one_hot(places(jnp.int32(group)), across, down)

    sorted_q = jnp.dot(pick, query[...], preferred_element_type=jnp.float32).astype(jnp.bfloat16)
    fkv[...] = jnp.dot(pick, fresh[...], preferred_element_type=jnp.float32).astype(jnp.bfloat16)
    for h in range(16):
        for d in range(NI):
            q[d, h * 16 : (h + 1) * 16, :] = sorted_q[d * 16 : (d + 1) * 16, h * 128 : (h + 1) * 128]
    in_row = lax.broadcasted_iota(jnp.int32, (256, 128), 0) % 4
    flag = [jnp.where(lengths[in_req[d]] == LONGEST, 1, 0) for d in range(NI)]
    qx[...] = jnp.zeros_like(qx)
    pos[NI] = jnp.zeros((256, 128), jnp.int32)
    for d in range(NI):
        seen = [jnp.int32(0)] * 4
        for n, (place, rank) in enumerate(here):
            seen = [jnp.where((place == d) & (rank == m), positions[i * 16 + n], seen[m]) for m in range(4)]
        pos[d] = functools.reduce(lambda x, m: jnp.where(in_row == m, seen[m], x), range(1, 4), jnp.full((256, 128), seen[0]))
        pos[NI] += pos[d] * flag[d]
        qx[...] = jnp.where(jnp.full((256, 128), flag[d]) == 1, q[d].astype(jnp.float32), qx[...])

    slot_of = lax.broadcasted_iota(jnp.int32, (384, 512), 0)
    j = lax.broadcasted_iota(jnp.int32, (1, 512), 1)
    k, dt = j // 32, (t - j // 4 + 2 * 512) % NT
    found = jnp.full((384, 512), -1, jnp.int32)
    for d in range(NI):
        page = jnp.where(k < NEAR, (d * NEAR + k) * NT + dt, (NI * NEAR + k - NEAR) * NT + dt)
        goes = (j % NL == l) & (j * 64 < lengths[in_req[d]])
        to = jnp.where(goes, target_v[pl.ds(in_req[d], 1), :] - (i * NL + l) * SLOTS, -1)
        found = jnp.where(slot_of == to, page, found)
    found = jnp.max(found, axis=1, keepdims=True)
    found = jnp.where(found < 0, (NI * NEAR + FAR) * NT, found)
    eye = lax.broadcasted_iota(jnp.int32, (128, 128), 0) == lax.broadcasted_iota(jnp.int32, (128, 128), 1)
    for n in range(3):
        column_n = jnp.broadcast_to(found[n * 128 : (n + 1) * 128], (128, 128))
        index[n : n + 1, :] = jnp.sum(jnp.where(eye, column_n, 0), axis=0, keepdims=True)
    zero[...] = jnp.zeros_like(zero)
    zero_out = pltpu.make_async_copy(zero, pages.at[NI * NEAR + FAR], own_sem.at[NEAR])
    zero_out.start()

    def update(m, total, weighted, s, v):
        top = jnp.maximum(m, jnp.max(s, axis=1, keepdims=True))
        shrink = jnp.exp(m - top)
        p = jnp.exp(s - top)
        total = total * shrink + jnp.sum(p, axis=1, keepdims=True)
        weighted = weighted * shrink + jnp.dot(p.astype(jnp.bfloat16), v, preferred_element_type=jnp.float32)
        return top, total, weighted

    def dots(a, b):
        return lax.dot_general(a, b, (((1,), (1,)), ((), ())), preferred_element_type=jnp.float32) * scale

    ext_copy.wait()
    ext_out = pltpu.make_async_copy(ext, pages.at[pl.ds(NI * NEAR, FAR)], ext_sem)
    ext_out.start()

    def extra_step(k, carry):
        n = lax.broadcasted_iota(jnp.int32, (1, NT * 64), 1)
        ts = (t + NT - n // 64) % NT
        token = (((NEAR + k) * NT + ts) * NL + l) * 64 + n % 64
        s = dots(qx[...].astype(jnp.bfloat16), ext[k, :, 0].reshape(NT * 64, 128))
        s = jnp.where(token < pos[NI, :, :1], s, MASKED)
        return update(*carry, s, ext[k, :, 1].reshape(NT * 64, 128))

    empty = (
        jnp.full((256, 1), LOW, jnp.float32),
        jnp.zeros((256, 1), jnp.float32),
        jnp.zeros((256, 128), jnp.float32),
    )
    mx, tx, ax = lax.fori_loop(0, FAR, extra_step, empty)

    a = lax.broadcasted_iota(jnp.int32, (256, 16), 0)
    b = lax.broadcasted_iota(jnp.int32, (256, 16), 1)
    visible = (a % 4 == b % 4) & (b // 4 <= (a // 4) % 4) & (l == 0)
    for d in range(NI):
        rows = slice(d * 16, (d + 1) * 16)
        s = jnp.where(visible, dots(q[d], fkv[rows, :128]), MASKED)
        far = jnp.full((256, 1), flag[d]) == 1
        start = (jnp.where(far, mx, LOW), jnp.where(far, tx, 0.0), jnp.where(far, ax, 0.0))
        m, total, weighted = update(*start, s, fkv[rows, 128:])
        acc[d] = weighted
        ml[d, :, :64] = jnp.broadcast_to(m, (256, 64))
        ml[d, :, 64:] = jnp.broadcast_to(total, (256, 64))

    def drain(n, c):
        each(n, lambda c: c.wait_send())
        for half in range(2):
            d = n // NEAR + 2 * half
            pltpu.make_async_copy(recv.at[d, n % NEAR], pages.at[d * NEAR + n % NEAR], page_sem.at[d, n % NEAR]).wait()
        return c

    def visit(n, c):
        k = n % NEAR
        each(n, lambda c: c.wait_recv())

        @pl.when(n < NEAR)
        def _():
            own_copy(k).wait()

        @pl.when(n + AHEAD < 2 * NEAR)
        def _():
            issue(n + AHEAD, 0)

        def request(half, c):
            d = n // NEAR + 2 * half
            pltpu.make_async_copy(recv.at[d, k], pages.at[d * NEAR + k], page_sem.at[d, k]).start()
            column = lax.broadcasted_iota(jnp.int32, (1, NT * 64), 1)
            ts = (t + NT - column // 64) % NT
            token = ((k * NT + ts) * NL + l) * 64 + column % 64
            s = dots(q[d], recv[d, k, :, 0].reshape(NT * 64, 128))
            s = jnp.where(token < pos[d, :, :1], s, MASKED)
            m, total, weighted = update(
                ml[d, :, :1], ml[d, :, 64:65], acc[d], s, recv[d, k, :, 1].reshape(NT * 64, 128)
            )
            acc[d] = weighted
            ml[d, :, :64] = jnp.broadcast_to(m, (256, 64))
            ml[d, :, 64:] = jnp.broadcast_to(total, (256, 64))
            return c

        lax.fori_loop(0, 2, request, 0)

        @pl.when(n >= NEAR)
        def _():
            drain(n - NEAR, 0)

        return c

    eye = lax.broadcasted_iota(jnp.int32, (64, 128), 0) == lax.broadcasted_iota(jnp.int32, (64, 128), 1)

    def send_parts(stage):
        for half in range(2):
            d = stage + 2 * half
            for n in range(NL):
                rows = slice(n * 64, (n + 1) * 64)
                give[stage, n, half * 64 : (half + 1) * 64, :] = acc[d, rows, :]
                for part in range(2):
                    stat = jnp.where(eye, ml[d, rows, part * 64 : part * 64 + 1], 0.0)
                    row = 128 + half * 2 + part
                    give[stage, n, row : row + 1, :] = jnp.sum(stat, axis=0, keepdims=True)
        copies = []
        for dl in range(1, NL):
            to = column(0, dl)
            copies.append(
                pltpu.make_async_remote_copy(
                    src_ref=give.at[stage, to[1]],
                    dst_ref=got.at[stage, dl - 1],
                    send_sem=s1_sem.at[stage, dl - 1],
                    recv_sem=r1_sem.at[stage, dl - 1],
                    device_id=to,
                    device_id_type=MESH,
                )
            )
        for c in copies:
            c.start()
        return copies

    def by_x(stage, half):
        return stage == 0 or half == 0

    def spread(stage, half, phase, rows):
        along_x = by_x(stage, half) == (phase == 0)
        copies = []
        for n in range(1, NI):
            copies.append(
                pltpu.make_async_remote_copy(
                    src_ref=rows,
                    dst_ref=rows,
                    send_sem=s2_sem.at[stage, half, phase, n],
                    recv_sem=r2_sem.at[stage, half, phase, n],
                    device_id=column(n, 0) if along_x else column(0, n),
                    device_id_type=MESH,
                )
            )
        for c in copies:
            c.start()
        return copies


    def join(stage, copies):
        for c in copies:
            c.wait_recv()
        sent = []
        blocks = [give.at[stage, l]] + [got.at[stage, n] for n in range(NL - 1)]
        for half in range(2):

            def stat(block, part):
                row = 128 + half * 2 + part
                return jnp.sum(jnp.where(eye, block[row : row + 1, :], 0.0), axis=1, keepdims=True)

            tops = [stat(block, 0) for block in blocks]
            top = functools.reduce(jnp.maximum, tops)
            shares = [jnp.exp(x - top) for x in tops]
            total = sum(stat(block, 1) * share for block, share in zip(blocks, shares))
            weighted = sum(block[half * 64 : (half + 1) * 64, :] * share for block, share in zip(blocks, shares))
            joined = (weighted / total).astype(jnp.bfloat16)
            mine = l * NI + i if by_x(stage, half) else i * NL + l
            for h in range(4):
                ctx[stage, half, mine, :, h * 128 : (h + 1) * 128] = joined[h * 16 : (h + 1) * 16]
            sent.append(spread(stage, half, 0, ctx.at[stage, half, mine]))
        return sent

    def widen(stage, sent):
        wide = []
        for half in range(2):
            for c in sent[half]:
                c.wait_recv()
            at = l * NI if by_x(stage, half) else i * NL
            wide.append(spread(stage, half, 1, ctx.at[stage, half, pl.ds(at, NI)]))
        return wide

    def project(stage, wide):
        for c in wide[0] + wide[1]:
            c.wait_recv()

        def block(group, half, n):
            return ctx[stage, half, n * NI + group if by_x(stage, half) else group * NL + n]

        context = jnp.concatenate(
            [
                jnp.concatenate([block(group, half, n) for n in range(NL)], axis=1)
                for group in range(NI)
                for half in range(2)
            ],
            axis=0,
        )

        def sum_copy(dt):
            to = plane(0, dt)
            return pltpu.make_async_remote_copy(
                src_ref=proj.at[stage, to[2]],
                dst_ref=red.at[stage, dt - 1],
                send_sem=s4_sem.at[stage, dt - 1],
                recv_sem=r4_sem.at[stage, dt - 1],
                device_id=to,
                device_id_type=MESH,
            )

        core = lax.rem(t, 2)
        for n in range(NT // 2):
            chip = lax.rem(t // 2 + n, NT // 2)
            columns = pl.ds(pl.multiple_of(chip * 256, 256), 256)
            out = jnp.dot(context, w[:, columns], preferred_element_type=jnp.float32)
            proj[stage, 2 * chip] = out[:, :128]
            proj[stage, 2 * chip + 1] = out[:, 128:]
            if n:
                for c in range(2):
                    sum_copy(2 * n - core + c).start()
            else:
                sum_copy(1 + 6 * core).start()
        return [sum_copy(dt) for dt in range(1, NT)]

    def reduce(stage, copies):
        total = proj[stage, t]
        for n, c in enumerate(copies):
            c.wait_recv()
            total = total + red[stage, n]
        return total

    lax.fori_loop(0, 6, visit, 0)
    parts = [send_parts(0)]
    lax.fori_loop(6, 7, visit, 0)
    contexts = join(0, parts[0])
    lax.fori_loop(7, 8, visit, 0)
    wide = widen(0, contexts)
    contexts += wide
    lax.fori_loop(8, 10, visit, 0)
    w_copy.wait()
    sums = [project(0, wide)]
    lax.fori_loop(10, 12, visit, 0)
    parts.append(send_parts(1))
    first = reduce(0, sums[0])
    lax.fori_loop(6, 9, drain, 0)
    sent = join(1, parts[1])
    for copies in [zero_out, ext_out]:
        copies.wait()
    for copies in parts + contexts:
        for c in copies:
            c.wait_send()
    wide = widen(1, sent)
    lax.fori_loop(9, 12, drain, 0)
    sums.append(project(1, wide))
    for copies in sent + wide:
        for c in copies:
            c.wait_send()
    second = reduce(1, sums[1])

    for group in range(NI):
        value = jnp.concatenate([(first, second)[d % 2][group * 32 + d // 2 * 16 :][:16] for d in range(NI)], axis=0)
        ordered = jnp.zeros((64, 128), jnp.float32)
        for _ in range(3):
            piece = value.astype(jnp.bfloat16)
            value = value - piece.astype(jnp.float32)
            ordered += jnp.dot(back[group], piece, preferred_element_type=jnp.float32)
        own_rows = slice(group * 16, (group + 1) * 16)
        for step in range(4):
            attn[step, own_rows] = ordered[step * 16 : (step + 1) * 16] + residual[step, own_rows].astype(jnp.float32)

    for copies in sums:
        for c in copies:
            c.wait_send()


def run_main(*args):
    hbm, vmem, smem = (pl.BlockSpec(memory_space=m) for m in (pl.ANY, pltpu.VMEM, pltpu.SMEM))
    bf, f32, i32, dma = jnp.bfloat16, jnp.float32, jnp.int32, pltpu.SemaphoreType.DMA
    return pl.pallas_call(
        main_kernel,
        out_shape=(
            jax.ShapeDtypeStruct((NI * NEAR + FAR + 1, NT, 2, 64, 128), bf),
            jax.ShapeDtypeStruct((4, 64, 128), f32),
            jax.ShapeDtypeStruct((3, 128), i32),
        ),
        in_specs=[smem] * 5 + [hbm, hbm, pl.BlockSpec(memory_space=pltpu.HBM)] + [vmem] * 4,
        out_specs=(hbm, vmem, vmem),
        scratch_shapes=[
            pltpu.VMEM((SRC, 2, NT, 64, 128), bf),
            pltpu.VMEM((NI, NEAR, 2, NT, 64, 128), bf),
            pltpu.VMEM((NI, NEAR, NT, 2, 64, 128), bf),
            pltpu.VMEM((FAR, NT, 2, 64, 128), bf),
            pltpu.VMEM((2048, 1024), bf),
            pltpu.VMEM((NI, 256, 128), bf),
            pltpu.VMEM((256, 128), f32),
            pltpu.VMEM((64, 256), bf),
            pltpu.VMEM((NI + 1, 256, 128), i32),
            pltpu.VMEM((NI, 256, 128), f32),
            pltpu.VMEM((NI, 256, 128), f32),
            pltpu.VMEM((NI, 64, 64), bf),
            pltpu.SMEM((NI,), i32),
            pltpu.VMEM((2, NL, 136, 128), f32),
            pltpu.VMEM((2, NL - 1, 136, 128), f32),
            pltpu.VMEM((2, 2, NI * NL, 16, 512), bf),
            pltpu.VMEM((2, NT, 128, 128), f32),
            pltpu.VMEM((2, NT - 1, 128, 128), f32),
            pltpu.VMEM((NT, 2, 64, 128), bf),
            dma((NI, NEAR, NT)),
            dma((NI, NEAR, NT)),
            dma((NEAR + 1,)),
            dma((NI, NEAR)),
            dma,
            dma,
            dma,
            dma((2, NL - 1)),
            dma((2, NL - 1)),
            dma((2, 2, 2, NI)),
            dma((2, 2, 2, NI)),
            dma((2, NT - 1)),
            dma((2, NT - 1)),
        ],
        compiler_params=pltpu.CompilerParams(
            collective_id=0, has_side_effects=True, vmem_limit_bytes=40 * 1024 * 1024
        ),
    )(*args)


def place_kernel(index, pages, pool, sem):
    def place(s, c):
        pltpu.make_async_copy(pages.at[index[s // 128, s % 128]], pool.at[s], sem).start()
        return c

    lax.fori_loop(0, SLOTS, place, 0, unroll=8)
    pltpu.make_async_copy(pool, pool, sem).wait()


def place_pages(index, pages):
    smem, hbm = pl.BlockSpec(memory_space=pltpu.SMEM), pl.BlockSpec(memory_space=pl.ANY)
    return pl.pallas_call(
        place_kernel,
        out_shape=jax.ShapeDtypeStruct((SLOTS, 2, 64, 128), jnp.bfloat16),
        in_specs=[smem, hbm],
        out_specs=hbm,
        scratch_shapes=[pltpu.SemaphoreType.DMA],
        compiler_params=pltpu.CompilerParams(vmem_limit_bytes=12 * 1024 * 1024),
    )(index, pages)


def shards(
    prefill_pool,
    lengths,
    src_table,
    dst_table,
    row_request,
    positions,
    queries,
    step_key_value,
    out_weight,
    residual,
):
    src, dst = src_table[:, 0], dst_table[:, 0]
    route = sum((src >= n * GROUP).astype(jnp.int32) * NI + (dst >= n * GROUP).astype(jnp.int32) for n in range(1, NI))
    extra = lax.switch(
        jnp.sum(jnp.where(lengths == LONGEST, route, 0)),
        [functools.partial(move_extra, p, g) for p in range(NI) for g in range(NI)],
        lengths,
        src_table,
        prefill_pool,
    )
    pages, attn, index = run_main(
        src_table,
        dst_table,
        lengths,
        row_request,
        positions,
        prefill_pool,
        extra,
        out_weight,
        dst_table,
        queries.reshape(64, 2048),
        step_key_value.reshape(64, 256),
        residual,
    )
    pool = place_pages(index, pages.reshape((NI * NEAR + FAR + 1) * NT, 2, 64, 128))
    return pool.reshape(SLOTS, 2, 1, 64, 128), attn


def solution(mesh):
    in_specs = (
        P(("instance", "layout", "tensor"), None, None, None, None),
        P(),
        P(),
        P(),
        P(),
        P(),
        P(None, "instance", "tensor"),
        P(None, "instance", None, "tensor", None),
        P("tensor", ("instance", "layout")),
        P(None, None, ("instance", "layout", "tensor")),
    )
    out_specs = (
        P(("instance", "layout"), None, "tensor", None, None),
        P(None, None, ("instance", "layout", "tensor")),
    )
    return jax.shard_map(shards, mesh=mesh, in_specs=in_specs, out_specs=out_specs, check_vma=False)
```
